256 devices in a mesh: depth: 8 (over x, z_hi), pos: 32 (over y, z_lo, core).
Axes of the slice: x: 4, y: 4, z: 8 (z_hi: 2, z_lo: 4; z = z_hi * 4 + z_lo), core: 2. Of those that a mesh axis runs over, the one named last changes fastest.
Arguments:
- object_slices: bfloat16 [8, 256, 2, 256], P('depth', 'pos'), may hold values from -1 to 2, as said below
- probe_wave: float32 [2, 128, 128], replicated, may hold values from -6 to 6
- propagator_phase: float32 [128, 128], replicated, may hold values from -3.140625 to 3.140625
- measured: float32 [1024, 128, 128], P(('depth', 'pos')), may hold values from 0.5 to 4
- offsets: int32 [1024, 2], P(('depth', 'pos')), may hold values from 0 to 128
- slice_order: int32 [8], replicated, may hold values from 0 to 7, each once
Outputs:
- object_grad: float32 [8, 256, 2, 256], P('depth', 'pos')
The draws below stay inside these ranges and needn't reach their ends.
Inputs may be any that keep to these rules, and one draw needn't show every extreme that they name: `object_slices`: the real parts lie around 1 and the imaginary parts around 0.
All inputs are finite; a program needn't handle non-finite values.
Results may differ from the reference program's by a relative error of at most 0.0003.
Values may be sent and summed in bfloat16 or wider, within the bound.
A program may use at most 128 MiB of HBM per device.

```python
import math
import jax
import jax.numpy as jnp
from jax import lax

PROBE = 128
OBJ = 256
P_DEV = 4
SLICES = 8
POSITIONS = 1024


def draw_object_slices(key, part):
    key = jax.random.fold_in(key, 11)
    shape = (SLICES, OBJ, 2, OBJ)
    noise = 0.2 * jnp.clip(jax.random.normal(key, shape, jnp.float32), -4.0, 4.0)
    centre = jnp.array([1.0, 0.0], jnp.float32).reshape(1, 1, 2, 1)
    return (centre + noise).astype(jnp.bfloat16)


def plant(result, key, smallest, largest):
    shape = result.shape
    index_at = [jax.random.randint(jax.random.fold_in(key, axis), (), 0, shape[axis]) for axis in range(len(shape))]
    result = result.at[tuple(index_at)].set(smallest)
    longest = shape.index(max(shape))
    index_at[longest] = (index_at[longest] + 1) % shape[longest]
    return result.at[tuple(index_at)].set(largest)


def block_levels(rng, shape, shards, smallest, top_value):
    loudness = 1.0
    for position, blocks in shards:
        steps = jax.random.uniform(jax.random.fold_in(jax.random.fold_in(rng, 6), position), (blocks,), jnp.float32, smallest / len(shards), top_value / len(shards))
        loudness = loudness * jnp.repeat(jnp.exp(steps), shape[position] // blocks).reshape((-1,) + (1,) * (len(shape) - 1 - position))
    return loudness


def gaussian(key, dims, scale, reach, dtype=jnp.bfloat16):
    values = scale * jax.random.normal(key, dims, jnp.float32)
    return jnp.clip(values, min=-reach, max=reach).astype(dtype)


def setup_inputs(seed: int = 0) -> dict:
    keys = jax.random.split(jax.random.key(seed), 7)
    return {
        "object_slices": draw_object_slices(jax.random.fold_in(keys[6], 71), 0),
        "probe_wave": gaussian(keys[1], (2, PROBE, PROBE), 1.0, 6.0, jnp.float32),
        "propagator_phase": jnp.clip(jax.random.uniform(keys[2], (PROBE, PROBE), jnp.float32, -3.140625, 3.140625), -3.140625, 3.140625),
        "measured": jnp.clip(jnp.exp(math.log(4.0) - 2.0794415 * jax.random.uniform(keys[3], (POSITIONS, PROBE, PROBE), jnp.float32) ** block_levels(keys[3], (POSITIONS, PROBE, PROBE), ((0, 256),), -0.2, 0.2)), 0.5, 4.0),
        "offsets": plant(jax.random.randint(keys[4], (POSITIONS, 2), 0, OBJ - PROBE + 1), jax.random.fold_in(keys[4], 1), 0, OBJ - PROBE).astype(jnp.int32),
        "slice_order": jax.random.permutation(keys[5], SLICES).astype(jnp.int32),
    }


def reference(object_slices, probe_wave, propagator_phase, measured, offsets, slice_order):
    transmit = object_slices.astype(jnp.float32)
    kernel = jnp.cos(propagator_phase) + 1j * jnp.sin(propagator_phase)
    start_wave = probe_wave[0] + 1j * probe_wave[1]
    factor = 0.25 * OBJ / (PROBE * math.sqrt(POSITIONS))
    anchor = jnp.zeros((), jnp.int32)

    def single(field, corner, sample):
        window = lax.dynamic_slice(field, (anchor, corner[0], anchor, corner[1]), (SLICES, PROBE, 2, PROBE))
        window = jnp.take(window, slice_order, axis=0)
        wave = start_wave
        for layer in range(SLICES):
            local = window[layer, :, 0, :] + 1j * window[layer, :, 1, :]
            wave = local * wave
            if layer < SLICES - 1:
                wave = jnp.fft.ifft2(kernel * jnp.fft.fft2(wave, norm='ortho'), norm='ortho')
        farfield = jnp.fft.fft2(wave, norm='ortho')
        intensity = jnp.real(farfield) ** 2 + jnp.imag(farfield) ** 2
        return 0.5 * jnp.sum((intensity - sample) ** 2)

    def block_misfit(field, corners, samples):
        values = jax.vmap(lambda corner, sample: single(field, corner, sample))(corners, samples)
        return factor * jnp.sum(values)
    gradient_fn = jax.grad(block_misfit)
    block = 4 * P_DEV
    corner_blocks = offsets.reshape(POSITIONS // block, block, 2)
    sample_blocks = measured.reshape(POSITIONS // block, block, PROBE, PROBE)

    def step(total, pieces):
        return (total + gradient_fn(transmit, pieces[0], pieces[1]), None)
    total, unused = lax.scan(step, jnp.zeros_like(transmit), (corner_blocks, sample_blocks))
    return total
```

```python
import functools
import math

import jax
import jax.numpy as jnp
import ml_dtypes
import numpy as np
from jax import lax
from jax.experimental import pallas as pl
from jax.experimental.pallas import tpu as pltpu
from jax.sharding import PartitionSpec as P

BF16 = jnp.bfloat16
F32 = jnp.float32
X, ZH, Y, ZL = 4, 2, 4, 4
Z = ZH * ZL


class Place:
    def __init__(self):
        depth, pos = lax.axis_index("depth"), lax.axis_index("pos")
        self.depth = depth
        self.x, self.zh = depth // ZH, depth % ZH
        self.core = pos % 2
        self.yz = pos // 2
        self.y, self.zl = self.yz // ZL, self.yz % ZL
        self.z = self.zh * ZL + self.zl

    def device(self, x=None, y=None, z=None, core=None):
        x = self.x if x is None else x
        y = self.y if y is None else y
        z = self.z if z is None else z
        core = self.core if core is None else core
        return (x * ZH + z // ZL, (y * ZL + z % ZL) * 2 + core)

    def xs(self, d):
        return (self.x + d) % X

    def ys(self, d):
        return (self.y + d) % Y

    def zs(self, d):
        return (self.z + d) % Z


def greet(me):
    barrier = pltpu.get_barrier_semaphore()
    partners = [me.device(core=1 - me.core)]
    partners += [me.device(x=me.xs(d)) for d in range(1, X)]
    partners += [me.device(y=me.ys(d)) for d in range(1, Y)]
    partners += [me.device(z=me.zs(d)) for d in range(1, Z)]
    for device in partners:
        pl.semaphore_signal(barrier, inc=1, device_id=device, device_id_type=pl.DeviceIdType.MESH)
    pl.semaphore_wait(barrier, len(partners))


class Sender:
    def __init__(self, send, recv):
        self.send, self.recv, self.used, self.copies = send, recv, 0, []

    def start(self, src, dst, device):
        index = self.used
        self.used += 1
        copy = pltpu.make_async_remote_copy(
            src_ref=src, dst_ref=dst, send_sem=self.send.at[index], recv_sem=self.recv.at[index],
            device_id=device, device_id_type=pl.DeviceIdType.MESH)
        copy.start()
        self.copies.append(copy)
        return copy

    def drain(self):
        for copy in self.copies:
            copy.wait_send()


def gather_kernel(block_ref, out, send, recv):
    me = Place()
    x, y, c = me.x, me.y, me.core
    depth_line = pl.ds(ZH * x, ZH)
    yz_line = pl.ds(ZL * y, ZL)
    for half in range(2):
        out[half, me.depth, me.yz, c] = block_ref[:, half * 128:(half + 1) * 128]
    greet(me)
    net = Sender(send, recv)
    sibling = me.device(core=1 - c)

    def share(spot):
        return net.start(out.at[spot], out.at[spot], sibling)

    own = (slice(None), me.depth, me.yz, c)
    phase = [net.start(out.at[own], out.at[own], me.device(z=me.zs(d))) for d in (4, 3, 5, 2, 6, 1, 7)]
    for copy in phase:
        copy.wait_recv()

    spot_a = (0, depth_line, yz_line, c)
    spot_b = (1, depth_line, yz_line, c)
    phase_a = [net.start(out.at[spot_a], out.at[spot_a], me.device(x=me.xs(d))) for d in (2, 1, 3)]
    phase_b = [net.start(out.at[spot_b], out.at[spot_b], me.device(y=me.ys(d))) for d in (2, 1, 3)]
    for copy in phase_a:
        copy.wait_recv()
    unit_a = lambda yy, part=slice(None): (0, part, pl.ds(ZL * yy, ZL), c)
    unit_b = lambda xx, part=slice(None): (1, pl.ds(ZH * xx, ZH), part, c)
    a_up = net.start(out.at[unit_a(y)], out.at[unit_a(y)], me.device(y=me.ys(1)))
    a_down = net.start(out.at[unit_a(y)], out.at[unit_a(y)], me.device(y=me.ys(3)))
    for copy in phase_b:
        copy.wait_recv()
    b_up = net.start(out.at[unit_b(x)], out.at[unit_b(x)], me.device(x=me.xs(1)))
    b_down = net.start(out.at[unit_b(x)], out.at[unit_b(x)], me.device(x=me.xs(3)))
    shared = [share(unit_a(y)), share(unit_b(x))]
    low_d, high_d = pl.ds(0, 4), pl.ds(4, 4)
    low_y, high_y = pl.ds(0, 8), pl.ds(8, 8)
    a_up.wait_recv()
    spot = unit_a(me.ys(3), low_d)
    a_up2 = net.start(out.at[spot], out.at[spot], me.device(y=me.ys(1)))
    a_down.wait_recv()
    spot = unit_a(me.ys(1), high_d)
    a_down2 = net.start(out.at[spot], out.at[spot], me.device(y=me.ys(3)))
    b_up.wait_recv()
    spot = unit_b(me.xs(3), low_y)
    b_up2 = net.start(out.at[spot], out.at[spot], me.device(x=me.xs(1)))
    b_down.wait_recv()
    spot = unit_b(me.xs(1), high_y)
    b_down2 = net.start(out.at[spot], out.at[spot], me.device(x=me.xs(3)))
    shared += [share(unit_a(me.ys(3))), share(unit_a(me.ys(1))), share(unit_b(me.xs(3))), share(unit_b(me.xs(1)))]
    a_up2.wait_recv()
    shared.append(share(unit_a(me.ys(2), low_d)))
    a_down2.wait_recv()
    shared.append(share(unit_a(me.ys(2), high_d)))
    b_up2.wait_recv()
    shared.append(share(unit_b(me.xs(2), low_y)))
    b_down2.wait_recv()
    shared.append(share(unit_b(me.xs(2), high_y)))
    for copy in shared:
        copy.wait_recv()
    net.drain()


def gather(block):
    vmem = pl.BlockSpec(memory_space=pltpu.VMEM)
    copies = 7 + 6 + 4 + 4 + 10
    return pl.pallas_call(
        gather_kernel,
        out_shape=jax.ShapeDtypeStruct((2, X * ZH, Y * ZL, 2, 16, 128), BF16),
        in_specs=[vmem],
        out_specs=vmem,
        scratch_shapes=[pltpu.SemaphoreType.DMA((copies,)), pltpu.SemaphoreType.DMA((copies,))],
        compiler_params=pltpu.CompilerParams(collective_id=0, has_side_effects=True, vmem_limit_bytes=32 * 2**20),
    )(block)


def scatter_kernel(grad, out, acc, inbox, hop_a, hop_b, ring_a, ring_b, line_a, line_b, col, send, recv):
    me = Place()
    x, y, c = me.x, me.y, me.core
    other = 1 - c
    greet(me)
    net = Sender(send, recv)
    sibling = me.device(core=other)

    def unit_a(yy):
        return (0, slice(None), pl.ds(ZL * yy, ZL))

    def unit_b(xx):
        return (1, pl.ds(ZH * xx, ZH), slice(None))

    order = []
    for d in (2, 1, 3, 0):
        order += [unit_a(me.ys(d)), unit_b(me.xs(d))]
    first = [net.start(grad.at[u + (other,)], inbox.at[u], sibling) for u in order]

    def fold(i):
        first[i].wait_recv()
        u = order[i]
        acc[u] = grad[u + (c,)] + inbox[u]

    lo_a = lambda yy: (0, pl.ds(0, 4), pl.ds(ZL * yy, ZL))
    hi_a = lambda yy: (0, pl.ds(4, 4), pl.ds(ZL * yy, ZL))
    lo_b = lambda xx: (1, pl.ds(ZH * xx, ZH), pl.ds(0, 8))
    hi_b = lambda xx: (1, pl.ds(ZH * xx, ZH), pl.ds(8, 8))
    up_y, down_y = me.device(y=me.ys(1)), me.device(y=me.ys(3))
    up_x, down_x = me.device(x=me.xs(1)), me.device(x=me.xs(3))
    fold(0)
    a1 = net.start(acc.at[lo_a(me.ys(2))], hop_a.at[0], up_y)
    a2 = net.start(acc.at[hi_a(me.ys(2))], hop_a.at[1], down_y)
    fold(1)
    b1 = net.start(acc.at[lo_b(me.xs(2))], hop_b.at[0], up_x)
    b2 = net.start(acc.at[hi_b(me.xs(2))], hop_b.at[1], down_x)
    fold(2)
    fold(3)
    a1.wait_recv()
    u = lo_a(me.ys(1))
    acc[u] = acc[u] + hop_a[0]
    a3 = net.start(acc.at[unit_a(me.ys(1))], ring_a.at[0], up_y)
    b1.wait_recv()
    u = lo_b(me.xs(1))
    acc[u] = acc[u] + hop_b[0]
    b3 = net.start(acc.at[unit_b(me.xs(1))], ring_b.at[0], up_x)
    fold(4)
    fold(5)
    a2.wait_recv()
    u = hi_a(me.ys(3))
    acc[u] = acc[u] + hop_a[1]
    a4 = net.start(acc.at[unit_a(me.ys(3))], ring_a.at[1], down_y)
    b2.wait_recv()
    u = hi_b(me.xs(3))
    acc[u] = acc[u] + hop_b[1]
    b4 = net.start(acc.at[unit_b(me.xs(3))], ring_b.at[1], down_x)
    fold(6)
    fold(7)
    a3.wait_recv()
    a4.wait_recv()
    u = unit_a(y)
    acc[u] = acc[u] + ring_a[0] + ring_a[1]
    go_a = []
    for slot, d in enumerate((2, 1, 3)):
        u = (0, pl.ds(ZH * me.xs(d), ZH), pl.ds(ZL * y, ZL))
        go_a.append(net.start(acc.at[u], line_a.at[slot], me.device(x=me.xs(d))))
    b3.wait_recv()
    b4.wait_recv()
    u = unit_b(x)
    acc[u] = acc[u] + ring_b[0] + ring_b[1]
    go_b = []
    for slot, d in enumerate((2, 1, 3)):
        u = (1, pl.ds(ZH * x, ZH), pl.ds(ZL * me.ys(d), ZL))
        go_b.append(net.start(acc.at[u], line_b.at[slot], me.device(y=me.ys(d))))
    for copy in go_a:
        copy.wait_recv()
    u = (0, pl.ds(ZH * x, ZH), pl.ds(ZL * y, ZL))
    acc[u] = acc[u] + (line_a[0] + line_a[1]) + line_a[2]
    for copy in go_b:
        copy.wait_recv()
    u = (1, pl.ds(ZH * x, ZH), pl.ds(ZL * y, ZL))
    acc[u] = acc[u] + (line_b[0] + line_b[1]) + line_b[2]
    last = []
    for slot, d in enumerate((4, 3, 5, 2, 6, 1, 7)):
        z = me.zs(d)
        u = (slice(None), ZH * x + z // ZL, ZL * y + z % ZL)
        last.append(net.start(acc.at[u], col.at[slot], me.device(z=z)))
    total = acc[:, me.depth, me.yz]
    for slot, copy in enumerate(last):
        copy.wait_recv()
        total = total + col[slot]
    for half in range(2):
        out[:, half * 128:(half + 1) * 128] = total[half]
    net.drain()


def scatter(grad):
    vmem = pl.BlockSpec(memory_space=pltpu.VMEM)
    copies = 8 + 8 + 6 + 7
    return pl.pallas_call(
        scatter_kernel,
        out_shape=jax.ShapeDtypeStruct((16, 256), F32),
        in_specs=[vmem],
        out_specs=vmem,
        scratch_shapes=[
            pltpu.VMEM((2, 8, 16, 16, 128), F32),
            pltpu.VMEM((2, 8, 16, 16, 128), F32),
            pltpu.VMEM((2, 4, 4, 16, 128), F32),
            pltpu.VMEM((2, 2, 8, 16, 128), F32),
            pltpu.VMEM((2, 8, 4, 16, 128), F32),
            pltpu.VMEM((2, 2, 16, 16, 128), F32),
            pltpu.VMEM((3, 2, 4, 16, 128), F32),
            pltpu.VMEM((3, 2, 4, 16, 128), F32),
            pltpu.VMEM((7, 2, 16, 128), F32),
            pltpu.SemaphoreType.DMA((copies,)), pltpu.SemaphoreType.DMA((copies,))],
        compiler_params=pltpu.CompilerParams(collective_id=1, has_side_effects=True, vmem_limit_bytes=32 * 2**20),
    )(grad)


def dft_tables(length):
    index = np.arange(length)
    angle = -2.0 * np.pi / length * ((index[:, None] * index[None, :]) % length)
    real, imag = np.cos(angle) / math.sqrt(length), np.sin(angle) / math.sqrt(length)
    full = np.block([[real, imag], [-imag, real]])
    pairs = []
    for matrix in (full, full.T):
        high = matrix.astype(ml_dtypes.bfloat16)
        low = (matrix - high.astype(np.float64)).astype(ml_dtypes.bfloat16)
        pairs.append(np.stack([high, low]))
    return np.stack(pairs)


def split(value):
    high = value.astype(BF16)
    return high, (value - high.astype(F32)).astype(BF16)


def dot(left, right):
    return jnp.dot(left, right, preferred_element_type=F32)


def compute_kernel(factor, group, offsets_ref, order_ref, whole_ref, probe_ref, cos_ref, sin_ref,
                   measured_ref, table_ref, grad_ref, slab, windows, waves, back):
    halves, layers, rows2, lanes = whole_ref.shape
    length = probe_ref.shape[1]
    count = measured_ref.shape[0]
    groups = [tuple(range(first, first + group)) for first in range(0, count, group)]
    lane = lax.broadcasted_iota(jnp.int32, (length, lanes), 1)

    def right_map(blocks, which):
        high_table, low_table = table_ref[which, 0], table_ref[which, 1]
        stacked = jnp.concatenate([jnp.concatenate(pair, axis=1) for pair in blocks], axis=0)
        high, low = split(stacked)
        out = dot(high, high_table) + (dot(low, high_table) + dot(high, low_table))
        return [
            (out[i * length:(i + 1) * length, :length], out[i * length:(i + 1) * length, length:])
            for i in range(len(blocks))
        ]

    def left_map(blocks, which):
        high_table, low_table = table_ref[which, 0], table_ref[which, 1]
        stacked = jnp.concatenate([jnp.concatenate(pair, axis=0) for pair in blocks], axis=1)
        high, low = split(stacked)
        out = dot(high_table, high) + (dot(high_table, low) + dot(low_table, high))
        return [
            (out[:length, i * length:(i + 1) * length], out[length:, i * length:(i + 1) * length])
            for i in range(len(blocks))
        ]

    def forward(blocks):
        return left_map(right_map(blocks, 0), 1)

    def inverse(blocks):
        return left_map(right_map(blocks, 1), 0)

    def times(a, b):
        return (a[0] * b[0] - a[1] * b[1], a[0] * b[1] + a[1] * b[0])

    def conj_times(a, b):
        return (a[0] * b[0] + a[1] * b[1], a[0] * b[1] - a[1] * b[0])

    def load_slab(layer):
        index = order_ref[layer]
        for half in range(halves):
            slab[half] = whole_ref[half, index].astype(F32)

    def load_window(layer, position):
        row, column = offsets_ref[position, 0], offsets_ref[position, 1]
        shift = lax.rem(lanes - column, lanes)
        keep = lane < lanes - column
        parts = []
        for part in range(2):
            first = slab[0, pl.ds(2 * row + part, length, stride=2), :]
            second = slab[1, pl.ds(2 * row + part, length, stride=2), :]
            window = jnp.where(keep, pltpu.roll(first, shift, 1), pltpu.roll(second, shift, 1))
            windows[layer, position, part] = window
            parts.append(window)
        return tuple(parts)

    def add_grad(layer, position, pair):
        index = order_ref[layer]
        row, column = offsets_ref[position, 0], offsets_ref[position, 1]
        shift = lax.rem(column, lanes)
        first = lane >= column
        for part in range(2):
            moved = pltpu.roll(pair[part], shift, 1)
            spot = pl.ds(2 * row + part, length, stride=2)
            grad_ref[0, index, spot, :] += jnp.where(first, moved, 0.0)
            grad_ref[1, index, spot, :] += jnp.where(first, 0.0, moved)

    grad_ref[...] = jnp.zeros_like(grad_ref)
    for position in range(count):
        waves[0, position] = probe_ref[...]

    def wave_of(layer, position):
        return waves[layer, position, 0], waves[layer, position, 1]

    @pl.loop(0, layers - 1)
    def _(layer):
        load_slab(layer)
        medium = (cos_ref[...], sin_ref[...])
        for members in groups:
            blocks = [times(load_window(layer, p), wave_of(layer, p)) for p in members]
            blocks = [times(b, medium) for b in forward(blocks)]
            for p, pair in zip(members, inverse(blocks)):
                waves[layer + 1, p, 0] = pair[0]
                waves[layer + 1, p, 1] = pair[1]

    last = layers - 1
    load_slab(last)
    for members in groups:
        trans = [load_window(last, p) for p in members]
        blocks = [times(t, wave_of(last, p)) for t, p in zip(trans, members)]
        far = forward(blocks)
        scaled = []
        for pair, p in zip(far, members):
            miss = (2.0 * factor) * (pair[0] * pair[0] + pair[1] * pair[1] - measured_ref[p])
            scaled.append((miss * pair[0], miss * pair[1]))
        for p, t, pair in zip(members, trans, inverse(scaled)):
            add_grad(last, p, conj_times(wave_of(last, p), pair))
            pair = conj_times(t, pair)
            back[p, 0] = pair[0]
            back[p, 1] = pair[1]

    @pl.loop(0, layers - 1)
    def _(step):
        layer = layers - 2 - step
        medium = (cos_ref[...], sin_ref[...])
        for members in groups:
            blocks = [(back[p, 0], back[p, 1]) for p in members]
            blocks = [conj_times(medium, b) for b in forward(blocks)]
            for p, pair in zip(members, inverse(blocks)):
                add_grad(layer, p, conj_times(wave_of(layer, p), pair))
                pair = conj_times((windows[layer, p, 0], windows[layer, p, 1]), pair)
                back[p, 0] = pair[0]
                back[p, 1] = pair[1]


def compute(whole, probe, cosine, sine, measured, offsets, order, factor, group=2):
    halves, layers, rows2, lanes = whole.shape
    length = probe.shape[1]
    count = measured.shape[0]
    table = jnp.asarray(dft_tables(length))
    vmem = pl.BlockSpec(memory_space=pltpu.VMEM)
    smem = pl.BlockSpec(memory_space=pltpu.SMEM)
    return pl.pallas_call(
        functools.partial(compute_kernel, factor, group),
        out_shape=jax.ShapeDtypeStruct((halves, layers, rows2, lanes), F32),
        in_specs=[smem, smem] + [vmem] * 6,
        out_specs=vmem,
        scratch_shapes=[
            pltpu.VMEM((halves, rows2, lanes), F32),
            pltpu.VMEM((layers, count, 2, length, length), F32),
            pltpu.VMEM((layers, count, 2, length, length), F32),
            pltpu.VMEM((count, 2, length, length), F32),
        ],
        compiler_params=pltpu.CompilerParams(vmem_limit_bytes=48 * 2**20),
    )(offsets, order, whole, probe, cosine, sine, measured, table)


def per_device(object_slices, probe_wave, propagator_phase, measured, offsets, slice_order):
    width = object_slices.shape[3]
    length = probe_wave.shape[1]
    positions_total = offsets.shape[0] * lax.axis_size("depth") * lax.axis_size("pos")
    factor = 0.25 * width / (length * math.sqrt(positions_total))
    whole = gather(object_slices.reshape(16, width))
    grad = compute(
        whole.reshape(2, 8, 2 * width, 128), probe_wave, jnp.cos(propagator_phase), jnp.sin(propagator_phase),
        measured, offsets, slice_order, factor)
    total = scatter(grad.reshape(2, X * ZH, Y * ZL, 2, 16, 128))
    return total.reshape(object_slices.shape)


def solution(mesh):
    in_specs = (
        P("depth", "pos", None, None),
        P(),
        P(),
        P(("depth", "pos"), None, None),
        P(("depth", "pos"), None),
        P(),
    )
    out_specs = P("depth", "pos", None, None)
    return jax.shard_map(
        per_device, mesh=mesh, in_specs=in_specs, out_specs=out_specs, check_vma=False
    )
```

```python
import functools
import math

import jax
import jax.numpy as jnp
import ml_dtypes
import numpy as np
from jax import lax
from jax.experimental import pallas as pl
from jax.experimental.pallas import tpu as pltpu
from jax.sharding import PartitionSpec as P

BF16 = jnp.bfloat16
F32 = jnp.float32
X, ZH, Y, ZL = 4, 2, 4, 4
Z = ZH * ZL


class Place:
    def __init__(self):
        depth, pos = lax.axis_index("depth"), lax.axis_index("pos")
        self.depth = depth
        self.x, self.zh = depth // ZH, depth % ZH
        self.core = pos % 2
        self.yz = pos // 2
        self.y, self.zl = self.yz // ZL, self.yz % ZL
        self.z = self.zh * ZL + self.zl

    def device(self, x=None, y=None, z=None, core=None):
        x = self.x if x is None else x
        y = self.y if y is None else y
        z = self.z if z is None else z
        core = self.core if core is None else core
        return (x * ZH + z // ZL, (y * ZL + z % ZL) * 2 + core)

    def xs(self, d):
        return (self.x + d) % X

    def ys(self, d):
        return (self.y + d) % Y

    def zs(self, d):
        return (self.z + d) % Z


def greet(me):
    barrier = pltpu.get_barrier_semaphore()
    partners = [me.device(core=1 - me.core)]
    partners += [me.device(x=me.xs(d)) for d in range(1, X)]
    partners += [me.device(y=me.ys(d)) for d in range(1, Y)]
    partners += [me.device(z=me.zs(d)) for d in range(1, Z)]
    for device in partners:
        pl.semaphore_signal(barrier, inc=1, device_id=device, device_id_type=pl.DeviceIdType.MESH)
    pl.semaphore_wait(barrier, len(partners))


class Sender:
    def __init__(self, send, recv):
        self.send, self.recv, self.used, self.copies = send, recv, 0, []

    def start(self, src, dst, device):
        index = self.used
        self.used += 1
        copy = pltpu.make_async_remote_copy(
            src_ref=src, dst_ref=dst, send_sem=self.send.at[index], recv_sem=self.recv.at[index],
            device_id=device, device_id_type=pl.DeviceIdType.MESH)
        copy.start()
        self.copies.append(copy)
        return copy

    def drain(self):
        for copy in self.copies:
            copy.wait_send()


def gather_kernel(block_ref, out, send, recv):
    me = Place()
    x, y, c = me.x, me.y, me.core
    depth_line = pl.ds(ZH * x, ZH)
    yz_line = pl.ds(ZL * y, ZL)
    for half in range(2):
        out[half, me.depth, me.yz, c] = block_ref[:, half * 128:(half + 1) * 128]
    greet(me)
    net = Sender(send, recv)
    sibling = me.device(core=1 - c)

    def share(spot):
        return net.start(out.at[spot], out.at[spot], sibling)

    own = (slice(None), me.depth, me.yz, c)
    phase = [net.start(out.at[own], out.at[own], me.device(z=me.zs(d))) for d in (4, 3, 5, 2, 6, 1, 7)]
    for copy in phase:
        copy.wait_recv()

    spot_a = (0, depth_line, yz_line, c)
    spot_b = (1, depth_line, yz_line, c)
    phase_a = [net.start(out.at[spot_a], out.at[spot_a], me.device(x=me.xs(d))) for d in (2, 1, 3)]
    phase_b = [net.start(out.at[spot_b], out.at[spot_b], me.device(y=me.ys(d))) for d in (2, 1, 3)]
    for copy in phase_a:
        copy.wait_recv()
    unit_a = lambda yy, part=slice(None): (0, part, pl.ds(ZL * yy, ZL), c)
    unit_b = lambda xx, part=slice(None): (1, pl.ds(ZH * xx, ZH), part, c)
    a_up = net.start(out.at[unit_a(y)], out.at[unit_a(y)], me.device(y=me.ys(1)))
    a_down = net.start(out.at[unit_a(y)], out.at[unit_a(y)], me.device(y=me.ys(3)))
    for copy in phase_b:
        copy.wait_recv()
    b_up = net.start(out.at[unit_b(x)], out.at[unit_b(x)], me.device(x=me.xs(1)))
    b_down = net.start(out.at[unit_b(x)], out.at[unit_b(x)], me.device(x=me.xs(3)))
    shared = [share(unit_a(y)), share(unit_b(x))]
    low_d, high_d = pl.ds(0, 4), pl.ds(4, 4)
    low_y, high_y = pl.ds(0, 8), pl.ds(8, 8)
    a_up.wait_recv()
    spot = unit_a(me.ys(3), low_d)
    a_up2 = net.start(out.at[spot], out.at[spot], me.device(y=me.ys(1)))
    a_down.wait_recv()
    spot = unit_a(me.ys(1), high_d)
    a_down2 = net.start(out.at[spot], out.at[spot], me.device(y=me.ys(3)))
    b_up.wait_recv()
    spot = unit_b(me.xs(3), low_y)
    b_up2 = net.start(out.at[spot], out.at[spot], me.device(x=me.xs(1)))
    b_down.wait_recv()
    spot = unit_b(me.xs(1), high_y)
    b_down2 = net.start(out.at[spot], out.at[spot], me.device(x=me.xs(3)))
    shared += [share(unit_a(me.ys(3))), share(unit_a(me.ys(1))), share(unit_b(me.xs(3))), share(unit_b(me.xs(1)))]
    a_up2.wait_recv()
    shared.append(share(unit_a(me.ys(2), low_d)))
    a_down2.wait_recv()
    shared.append(share(unit_a(me.ys(2), high_d)))
    b_up2.wait_recv()
    shared.append(share(unit_b(me.xs(2), low_y)))
    b_down2.wait_recv()
    shared.append(share(unit_b(me.xs(2), high_y)))
    for copy in shared:
        copy.wait_recv()
    net.drain()


def gather(block):
    vmem = pl.BlockSpec(memory_space=pltpu.VMEM)
    copies = 7 + 6 + 4 + 4 + 10
    return pl.pallas_call(
        gather_kernel,
        out_shape=jax.ShapeDtypeStruct((2, X * ZH, Y * ZL, 2, 16, 128), BF16),
        in_specs=[vmem],
        out_specs=vmem,
        scratch_shapes=[pltpu.SemaphoreType.DMA((copies,)), pltpu.SemaphoreType.DMA((copies,))],
        compiler_params=pltpu.CompilerParams(collective_id=0, has_side_effects=True, vmem_limit_bytes=32 * 2**20),
    )(block)


def scatter_kernel(grad, out, acc, inbox, hop_a, hop_b, ring_a, ring_b, line_a, line_b, col, send, recv):
    me = Place()
    x, y, c = me.x, me.y, me.core
    other = 1 - c
    greet(me)
    net = Sender(send, recv)
    sibling = me.device(core=other)

    def unit_a(yy):
        return (0, slice(None), pl.ds(ZL * yy, ZL))

    def unit_b(xx):
        return (1, pl.ds(ZH * xx, ZH), slice(None))

    order = []
    for d in (2, 1, 3, 0):
        order += [unit_a(me.ys(d)), unit_b(me.xs(d))]
    first = [net.start(grad.at[u + (other,)], inbox.at[u], sibling) for u in order]

    def fold(i):
        first[i].wait_recv()
        u = order[i]
        acc[u] = grad[u + (c,)] + inbox[u]

    lo_a = lambda yy: (0, pl.ds(0, 4), pl.ds(ZL * yy, ZL))
    hi_a = lambda yy: (0, pl.ds(4, 4), pl.ds(ZL * yy, ZL))
    lo_b = lambda xx: (1, pl.ds(ZH * xx, ZH), pl.ds(0, 8))
    hi_b = lambda xx: (1, pl.ds(ZH * xx, ZH), pl.ds(8, 8))
    up_y, down_y = me.device(y=me.ys(1)), me.device(y=me.ys(3))
    up_x, down_x = me.device(x=me.xs(1)), me.device(x=me.xs(3))
    fold(0)
    a1 = net.start(acc.at[lo_a(me.ys(2))], hop_a.at[0], up_y)
    a2 = net.start(acc.at[hi_a(me.ys(2))], hop_a.at[1], down_y)
    fold(1)
    b1 = net.start(acc.at[lo_b(me.xs(2))], hop_b.at[0], up_x)
    b2 = net.start(acc.at[hi_b(me.xs(2))], hop_b.at[1], down_x)
    fold(2)
    fold(3)
    a1.wait_recv()
    u = lo_a(me.ys(1))
    acc[u] = acc[u] + hop_a[0]
    a3 = net.start(acc.at[unit_a(me.ys(1))], ring_a.at[0], up_y)
    b1.wait_recv()
    u = lo_b(me.xs(1))
    acc[u] = acc[u] + hop_b[0]
    b3 = net.start(acc.at[unit_b(me.xs(1))], ring_b.at[0], up_x)
    fold(4)
    fold(5)
    a2.wait_recv()
    u = hi_a(me.ys(3))
    acc[u] = acc[u] + hop_a[1]
    a4 = net.start(acc.at[unit_a(me.ys(3))], ring_a.at[1], down_y)
    b2.wait_recv()
    u = hi_b(me.xs(3))
    acc[u] = acc[u] + hop_b[1]
    b4 = net.start(acc.at[unit_b(me.xs(3))], ring_b.at[1], down_x)
    fold(6)
    fold(7)
    a3.wait_recv()
    a4.wait_recv()
    u = unit_a(y)
    acc[u] = acc[u] + ring_a[0] + ring_a[1]
    go_a = []
    for slot, d in enumerate((2, 1, 3)):
        u = (0, pl.ds(ZH * me.xs(d), ZH), pl.ds(ZL * y, ZL))
        go_a.append(net.start(acc.at[u], line_a.at[slot], me.device(x=me.xs(d))))
    b3.wait_recv()
    b4.wait_recv()
    u = unit_b(x)
    acc[u] = acc[u] + ring_b[0] + ring_b[1]
    go_b = []
    for slot, d in enumerate((2, 1, 3)):
        u = (1, pl.ds(ZH * x, ZH), pl.ds(ZL * me.ys(d), ZL))
        go_b.append(net.start(acc.at[u], line_b.at[slot], me.device(y=me.ys(d))))
    for copy in go_a:
        copy.wait_recv()
    u = (0, pl.ds(ZH * x, ZH), pl.ds(ZL * y, ZL))
    acc[u] = acc[u] + (line_a[0] + line_a[1]) + line_a[2]
    for copy in go_b:
        copy.wait_recv()
    u = (1, pl.ds(ZH * x, ZH), pl.ds(ZL * y, ZL))
    acc[u] = acc[u] + (line_b[0] + line_b[1]) + line_b[2]
    last = []
    for slot, d in enumerate((4, 3, 5, 2, 6, 1, 7)):
        z = me.zs(d)
        u = (slice(None), ZH * x + z // ZL, ZL * y + z % ZL)
        last.append(net.start(acc.at[u], col.at[slot], me.device(z=z)))
    total = acc[:, me.depth, me.yz]
    for slot, copy in enumerate(last):
        copy.wait_recv()
        total = total + col[slot]
    for half in range(2):
        out[:, half * 128:(half + 1) * 128] = total[half]
    net.drain()


def scatter(grad):
    vmem = pl.BlockSpec(memory_space=pltpu.VMEM)
    copies = 8 + 8 + 6 + 7
    return pl.pallas_call(
        scatter_kernel,
        out_shape=jax.ShapeDtypeStruct((16, 256), F32),
        in_specs=[vmem],
        out_specs=vmem,
        scratch_shapes=[
            pltpu.VMEM((2, 8, 16, 16, 128), F32),
            pltpu.VMEM((2, 8, 16, 16, 128), F32),
            pltpu.VMEM((2, 4, 4, 16, 128), F32),
            pltpu.VMEM((2, 2, 8, 16, 128), F32),
            pltpu.VMEM((2, 8, 4, 16, 128), F32),
            pltpu.VMEM((2, 2, 16, 16, 128), F32),
            pltpu.VMEM((3, 2, 4, 16, 128), F32),
            pltpu.VMEM((3, 2, 4, 16, 128), F32),
            pltpu.VMEM((7, 2, 16, 128), F32),
            pltpu.SemaphoreType.DMA((copies,)), pltpu.SemaphoreType.DMA((copies,))],
        compiler_params=pltpu.CompilerParams(collective_id=1, has_side_effects=True, vmem_limit_bytes=32 * 2**20),
    )(grad)


def dft_tables(length):
    index = np.arange(length)
    angle = -2.0 * np.pi / length * ((index[:, None] * index[None, :]) % length)
    real, imag = np.cos(angle) / math.sqrt(length), np.sin(angle) / math.sqrt(length)
    full = np.block([[real, imag], [-imag, real]])
    pairs = []
    for matrix in (full, full.T):
        high = matrix.astype(ml_dtypes.bfloat16)
        low = (matrix - high.astype(np.float64)).astype(ml_dtypes.bfloat16)
        pairs.append(np.stack([high, low]))
    return np.stack(pairs)


def split(value):
    high = value.astype(BF16)
    return high, (value - high.astype(F32)).astype(BF16)


def dot(left, right):
    return jnp.dot(left, right, preferred_element_type=F32)


def compute_kernel(factor, group, offsets_ref, order_ref, whole_ref, probe_ref, cos_ref, sin_ref,
                   measured_ref, table_ref, grad_ref, slab, windows, waves, back):
    halves, layers, rows2, lanes = whole_ref.shape
    length = probe_ref.shape[1]
    count = measured_ref.shape[0]
    groups = [tuple(range(first, first + group)) for first in range(0, count, group)]
    lane = lax.broadcasted_iota(jnp.int32, (length, lanes), 1)

    def right_map(blocks, which):
        high_table, low_table = table_ref[which, 0], table_ref[which, 1]
        results = []
        for pair in blocks:
            high, low = split(jnp.concatenate(pair, axis=1))
            out = dot(high, high_table) + (dot(low, high_table) + dot(high, low_table))
            results.append((out[:, :length], out[:, length:]))
        return results

    def left_map(blocks, which):
        high_table, low_table = table_ref[which, 0], table_ref[which, 1]
        stacked = jnp.concatenate([jnp.concatenate(pair, axis=0) for pair in blocks], axis=1)
        high, low = split(stacked)
        out = dot(high_table, high) + (dot(high_table, low) + dot(low_table, high))
        return [
            (out[:length, i * length:(i + 1) * length], out[length:, i * length:(i + 1) * length])
            for i in range(len(blocks))
        ]

    def forward(blocks):
        return left_map(right_map(blocks, 0), 1)

    def inverse(blocks):
        return left_map(right_map(blocks, 1), 0)

    def times(a, b):
        return (a[0] * b[0] - a[1] * b[1], a[0] * b[1] + a[1] * b[0])

    def conj_times(a, b):
        return (a[0] * b[0] + a[1] * b[1], a[0] * b[1] - a[1] * b[0])

    def load_slab(layer):
        index = order_ref[layer]
        for half in range(halves):
            slab[half] = whole_ref[half, index].astype(F32)

    def load_window(layer, position):
        row, column = offsets_ref[position, 0], offsets_ref[position, 1]
        shift = lax.rem(lanes - column, lanes)
        keep = lane < lanes - column
        parts = []
        for part in range(2):
            first = slab[0, pl.ds(2 * row + part, length, stride=2), :]
            second = slab[1, pl.ds(2 * row + part, length, stride=2), :]
            window = jnp.where(keep, pltpu.roll(first, shift, 1), pltpu.roll(second, shift, 1))
            windows[layer, position, part] = window
            parts.append(window)
        return tuple(parts)

    def add_grad(layer, position, pair):
        index = order_ref[layer]
        row, column = offsets_ref[position, 0], offsets_ref[position, 1]
        shift = lax.rem(column, lanes)
        first = lane >= column
        for part in range(2):
            moved = pltpu.roll(pair[part], shift, 1)
            spot = pl.ds(2 * row + part, length, stride=2)
            grad_ref[0, index, spot, :] += jnp.where(first, moved, 0.0)
            grad_ref[1, index, spot, :] += jnp.where(first, 0.0, moved)

    grad_ref[...] = jnp.zeros_like(grad_ref)
    for position in range(count):
        waves[0, position] = probe_ref[...]

    def wave_of(layer, position):
        return waves[layer, position, 0], waves[layer, position, 1]

    @pl.loop(0, layers - 1, unroll=7)
    def _(layer):
        load_slab(layer)
        medium = (cos_ref[...], sin_ref[...])
        for members in groups:
            blocks = [times(load_window(layer, p), wave_of(layer, p)) for p in members]
            blocks = [times(b, medium) for b in forward(blocks)]
            for p, pair in zip(members, inverse(blocks)):
                waves[layer + 1, p, 0] = pair[0]
                waves[layer + 1, p, 1] = pair[1]

    last = layers - 1
    load_slab(last)
    for members in groups:
        trans = [load_window(last, p) for p in members]
        blocks = [times(t, wave_of(last, p)) for t, p in zip(trans, members)]
        far = forward(blocks)
        scaled = []
        for pair, p in zip(far, members):
            miss = (2.0 * factor) * (pair[0] * pair[0] + pair[1] * pair[1] - measured_ref[p])
            scaled.append((miss * pair[0], miss * pair[1]))
        for p, t, pair in zip(members, trans, inverse(scaled)):
            add_grad(last, p, conj_times(wave_of(last, p), pair))
            pair = conj_times(t, pair)
            back[p, 0] = pair[0]
            back[p, 1] = pair[1]

    @pl.loop(0, layers - 1, unroll=7)
    def _(step):
        layer = layers - 2 - step
        medium = (cos_ref[...], sin_ref[...])
        for members in groups:
            blocks = [(back[p, 0], back[p, 1]) for p in members]
            blocks = [conj_times(medium, b) for b in forward(blocks)]
            for p, pair in zip(members, inverse(blocks)):
                add_grad(layer, p, conj_times(wave_of(layer, p), pair))
                pair = conj_times((windows[layer, p, 0], windows[layer, p, 1]), pair)
                back[p, 0] = pair[0]
                back[p, 1] = pair[1]


def compute(whole, probe, cosine, sine, measured, offsets, order, factor, group=4):
    halves, layers, rows2, lanes = whole.shape
    length = probe.shape[1]
    count = measured.shape[0]
    table = jnp.asarray(dft_tables(length))
    vmem = pl.BlockSpec(memory_space=pltpu.VMEM)
    smem = pl.BlockSpec(memory_space=pltpu.SMEM)
    return pl.pallas_call(
        functools.partial(compute_kernel, factor, group),
        out_shape=jax.ShapeDtypeStruct((halves, layers, rows2, lanes), F32),
        in_specs=[smem, smem] + [vmem] * 6,
        out_specs=vmem,
        scratch_shapes=[
            pltpu.VMEM((halves, rows2, lanes), F32),
            pltpu.VMEM((layers, count, 2, length, length), F32),
            pltpu.VMEM((layers, count, 2, length, length), F32),
            pltpu.VMEM((count, 2, length, length), F32),
        ],
        compiler_params=pltpu.CompilerParams(vmem_limit_bytes=48 * 2**20),
    )(offsets, order, whole, probe, cosine, sine, measured, table)


def per_device(object_slices, probe_wave, propagator_phase, measured, offsets, slice_order):
    width = object_slices.shape[3]
    length = probe_wave.shape[1]
    positions_total = offsets.shape[0] * lax.axis_size("depth") * lax.axis_size("pos")
    factor = 0.25 * width / (length * math.sqrt(positions_total))
    whole = gather(object_slices.reshape(16, width))
    grad = compute(
        whole.reshape(2, 8, 2 * width, 128), probe_wave, jnp.cos(propagator_phase), jnp.sin(propagator_phase),
        measured, offsets, slice_order, factor)
    total = scatter(grad.reshape(2, X * ZH, Y * ZL, 2, 16, 128))
    return total.reshape(object_slices.shape)


def solution(mesh):
    in_specs = (
        P("depth", "pos", None, None),
        P(),
        P(),
        P(("depth", "pos"), None, None),
        P(("depth", "pos"), None),
        P(),
    )
    out_specs = P("depth", "pos", None, None)
    return jax.shard_map(
        per_device, mesh=mesh, in_specs=in_specs, out_specs=out_specs, check_vma=False
    )
```

```python
import functools
import math

import jax
import jax.numpy as jnp
import ml_dtypes
import numpy as np
from jax import lax
from jax.experimental import pallas as pl
from jax.experimental.pallas import tpu as pltpu
from jax.sharding import PartitionSpec as P

BF16 = jnp.bfloat16
F32 = jnp.float32
X, ZH, Y, ZL = 4, 2, 4, 4
Z = ZH * ZL
MESH = pl.DeviceIdType.MESH


def dft_tables(length):
    index = np.arange(length)
    angle = -2.0 * np.pi / length * ((index[:, None] * index[None, :]) % length)
    real, imag = np.cos(angle) / math.sqrt(length), np.sin(angle) / math.sqrt(length)
    full = np.block([[real, imag], [-imag, real]])
    pairs = []
    for matrix in (full, full.T):
        high = matrix.astype(ml_dtypes.bfloat16)
        low = (matrix - high.astype(np.float64)).astype(ml_dtypes.bfloat16)
        pairs.append(np.stack([high, low]))
    return np.stack(pairs)


class Place:
    def __init__(self):
        depth, pos = lax.axis_index("depth"), lax.axis_index("pos")
        self.depth = depth
        self.x, self.zh = depth // ZH, depth % ZH
        self.core = pos % 2
        self.yz = pos // 2
        self.y, self.zl = self.yz // ZL, self.yz % ZL
        self.z = self.zh * ZL + self.zl

    def device(self, x=None, y=None, z=None, core=None):
        x = self.x if x is None else x
        y = self.y if y is None else y
        z = self.z if z is None else z
        core = self.core if core is None else core
        return (x * ZH + z // ZL, (y * ZL + z % ZL) * 2 + core)

    def xs(self, d):
        return (self.x + d) % X

    def ys(self, d):
        return (self.y + d) % Y

    def zs(self, d):
        return (self.z + d) % Z


def greet(me):
    barrier = pltpu.get_barrier_semaphore()
    partners = [me.device(core=1 - me.core)]
    partners += [me.device(x=me.xs(d)) for d in range(1, X)]
    partners += [me.device(y=me.ys(d)) for d in range(1, Y)]
    partners += [me.device(z=me.zs(d)) for d in range(1, Z)]
    for device in partners:
        pl.semaphore_signal(barrier, inc=1, device_id=device, device_id_type=MESH)
    pl.semaphore_wait(barrier, len(partners))


class Sender:
    def __init__(self, send, recv):
        self.send, self.recv, self.used, self.copies = send, recv, 0, []

    def start(self, src, dst, device):
        index = self.used
        self.used += 1
        copy = pltpu.make_async_remote_copy(
            src_ref=src, dst_ref=dst, send_sem=self.send.at[index], recv_sem=self.recv.at[index],
            device_id=device, device_id_type=MESH)
        copy.start()
        self.copies.append(copy)
        return copy

    def drain(self):
        for copy in self.copies:
            copy.wait_send()


GATHER_COPIES = 7 + 2 * (3 + 8 + 4) + 2 * 7


def gather_whole(me, net, out, meanwhile):
    x, y, c = me.x, me.y, me.core
    sibling = me.device(core=1 - c)

    def push(spot, device):
        return net.start(out.at[spot], out.at[spot], device)

    own = (slice(None), me.depth, me.yz, c)
    phase = [push(own, me.device(z=me.zs(d))) for d in (4, 3, 5, 2, 6, 1, 7)]
    meanwhile()
    for copy in phase:
        copy.wait_recv()

    def line(half, first, second):
        if half == 0:
            return (0, pl.ds(ZH * first, ZH), pl.ds(ZL * second, ZL), c)
        return (1, pl.ds(ZH * second, ZH), pl.ds(ZL * first, ZL), c)

    def unit(half, second):
        if half == 0:
            return (0, slice(None), pl.ds(ZL * second, ZL), c)
        return (1, pl.ds(ZH * second, ZH), slice(None), c)

    first = (me.xs, me.ys)
    second = (me.ys, me.xs)
    to_first = (lambda d: me.device(x=me.xs(d)), lambda d: me.device(y=me.ys(d)))
    to_second = (lambda d: me.device(y=me.ys(d)), lambda d: me.device(x=me.xs(d)))
    ups, downs, direct = [{}, {}], [{}, {}], [{}, {}]

    def spread(half, d):
        spot = line(half, first[half](d), second[half](0))
        ups[half][d] = push(spot, to_second[half](1))
        downs[half][d] = push(spot, to_second[half](3))

    for half in range(2):
        for d in (1, 3, 2):
            direct[half][d] = push(line(half, first[half](0), second[half](0)), to_first[half](d))
    for half in range(2):
        spread(half, 0)
    for d in (1, 3, 2):
        for half in range(2):
            direct[half][d].wait_recv()
            spread(half, 4 - d)
    shared = [push(unit(half, second[half](0)), sibling) for half in range(2)]
    relayed = []
    for d in (0, 3, 1, 2):
        for half in range(2):
            ups[half][d].wait_recv()
            if d in (0, 2):
                spot = line(half, first[half](d), second[half](3))
                relayed.append((half, d, push(spot, to_second[half](1))))
            downs[half][d].wait_recv()
            if d in (1, 3):
                spot = line(half, first[half](d), second[half](1))
                relayed.append((half, d, push(spot, to_second[half](3))))
    for half in range(2):
        shared.append(push(unit(half, second[half](3)), sibling))
        shared.append(push(unit(half, second[half](1)), sibling))
    for half, d, copy in relayed:
        copy.wait_recv()
        shared.append(push(line(half, first[half](d), second[half](2)), sibling))
    for copy in shared:
        copy.wait_recv()


def split(value):
    high = value.astype(BF16)
    return high, (value - high.astype(F32)).astype(BF16)


def dot(left, right):
    return jnp.dot(left, right, preferred_element_type=F32)


def times(a, b):
    return (a[0] * b[0] - a[1] * b[1], a[0] * b[1] + a[1] * b[0])


def conj_times(a, b):
    return (a[0] * b[0] + a[1] * b[1], a[0] * b[1] - a[1] * b[0])


def kernel(factor, offsets_ref, order_ref, block_ref, probe_hbm, phase_hbm, measured_hbm, table_hbm, out_ref,
           whole, probe_ref, phase_ref, measured_ref, table_ref, medium, slab, windows, waves, pend, place_ref,
           grads, inbox, acc, hop, ring, line, piece, stage, xbox, pair, zbox, final,
           load_sem, send, recv, s1_send, s1_recv, hop_send, hop_recv, ring_send, ring_recv, line_send, line_recv,
           end_send, end_recv):
    layers = order_ref.shape[0]
    count, length = measured_ref.shape[:2]
    lanes = whole.shape[-1]
    field = 2 * lanes
    me = Place()
    x, y, c = me.x, me.y, me.core
    other = 1 - c
    net = Sender(send, recv)
    loads = [
        pltpu.make_async_copy(src, dst, load_sem.at[i])
        for i, (src, dst) in enumerate((
            (phase_hbm, phase_ref), (probe_hbm, probe_ref), (table_hbm, table_ref), (measured_hbm, measured_ref)))
    ]
    for load in loads:
        load.start()
    for half in range(2):
        whole[half, me.depth, me.yz, c] = block_ref[:, half * lanes:(half + 1) * lanes]
    greet(me)
    lane = lax.broadcasted_iota(jnp.int32, (length, lanes), 1)

    def prepare():
        for load in loads:
            load.wait()
        medium[0] = jnp.cos(phase_ref[...])
        medium[1] = jnp.sin(phase_ref[...])
        rows = lax.broadcasted_iota(jnp.int32, (field, length), 0)
        inner = lax.broadcasted_iota(jnp.int32, (field, length), 1)
        for p in range(count):
            hit = rows - inner == offsets_ref[p, 0]
            place_ref[:, p * length:(p + 1) * length] = jnp.where(hit, 1.0, 0.0).astype(BF16)
            waves[0, p] = probe_ref[...]

    gather_whole(me, net, whole, prepare)

    def right_map(blocks, which):
        high_table, low_table = table_ref[which, 0], table_ref[which, 1]
        results = []
        for block in blocks:
            high, low = split(jnp.concatenate(block, axis=1))
            out = dot(high, high_table) + (dot(low, high_table) + dot(high, low_table))
            results.append((out[:, :length], out[:, length:]))
        return results

    def left_map(blocks, which):
        high_table, low_table = table_ref[which, 0], table_ref[which, 1]
        stacked = jnp.concatenate([jnp.concatenate(block, axis=0) for block in blocks], axis=1)
        high, low = split(stacked)
        out = dot(high_table, high) + (dot(high_table, low) + dot(low_table, high))
        return [
            (out[:length, i * length:(i + 1) * length], out[length:, i * length:(i + 1) * length])
            for i in range(len(blocks))
        ]

    def forward(blocks):
        return left_map(right_map(blocks, 0), 1)

    def inverse(blocks):
        return left_map(right_map(blocks, 1), 0)

    def load_windows(layer):
        index = order_ref[layer]
        for half in range(2):
            slab[half] = whole[half, index].reshape(2 * field, lanes).astype(F32)
        for p in range(count):
            row, column = offsets_ref[p, 0], offsets_ref[p, 1]
            shift = lax.rem(lanes - column, lanes)
            keep = lane < lanes - column
            for part in range(2):
                left = slab[0, pl.ds(2 * row + part, length, stride=2), :]
                right = slab[1, pl.ds(2 * row + part, length, stride=2), :]
                windows[layer, p, part] = jnp.where(keep, pltpu.roll(left, shift, 1), pltpu.roll(right, shift, 1))

    def window_of(layer, p):
        return windows[layer, p, 0], windows[layer, p, 1]

    def wave_of(layer, p):
        return waves[layer, p, 0], waves[layer, p, 1]

    def add_grads(j, slot):
        layer = layers - 1 - j
        terms = [conj_times(wave_of(layer, p), (pend[slot, p, 0], pend[slot, p, 1])) for p in range(count)]
        for part in range(2):
            moved = []
            for p in range(count):
                column = offsets_ref[p, 1]
                turned = pltpu.roll(terms[p][part], lax.rem(column, lanes), 1)
                moved.append(jnp.concatenate(
                    [jnp.where(lane >= column, turned, 0.0), jnp.where(lane >= column, 0.0, turned)], axis=1))
            high, low = split(jnp.concatenate(moved, axis=0))
            total = dot(place_ref[...], high) + dot(place_ref[...], low)
            for half in range(2):
                grads[j, half, part] = total[:, half * lanes:(half + 1) * lanes].reshape(Y * ZL, 2, 8, lanes)

    def remote(src, dst, send_sem, recv_sem, device):
        return pltpu.make_async_remote_copy(
            src_ref=src, dst_ref=dst, send_sem=send_sem, recv_sem=recv_sem, device_id=device, device_id_type=MESH)

    def y_unit(d):
        return pl.ds(ZL * me.ys(d), ZL)

    def share(j):
        return remote(grads.at[j, :, :, :, other], inbox.at[j], s1_send.at[j], s1_recv.at[j], me.device(core=other))

    def hop_of(j, side):
        return remote(acc.at[j, side, :, y_unit(2)], hop.at[j, side], hop_send.at[j, side], hop_recv.at[j, side],
                      me.device(y=me.ys(1 + 2 * side)))

    def ring_of(j, side):
        return remote(acc.at[j, :, :, y_unit(1 + 2 * side)], ring.at[j, side], ring_send.at[j, side],
                      ring_recv.at[j, side], me.device(y=me.ys(1 + 2 * side)))

    def lines(j):
        result = []
        for d in range(1, ZL):
            zl = (me.zl + d) % ZL
            result.append(remote(acc.at[j, :, :, ZL * y + zl], line.at[j, d - 1], line_send.at[j, d - 1],
                                 line_recv.at[j, d - 1], me.device(z=me.zh * ZL + zl)))
        return result

    def do_share(j):
        share(j).start()

    def do_fold(j):
        share(j).wait_recv()
        acc[j] = grads[j, :, :, :, c] + inbox[j]
        for side in range(2):
            hop_of(j, side).start()

    def do_ring(j):
        for side, d in ((0, 1), (1, 3)):
            hop_of(j, side).wait_recv()
            acc[j, side, :, y_unit(d)] = acc[j, side, :, y_unit(d)] + hop[j, side]
            ring_of(j, side).start()

    def do_line(j):
        for side in range(2):
            ring_of(j, side).wait_recv()
        acc[j, :, :, y_unit(0)] = acc[j, :, :, y_unit(0)] + ring[j, 0] + ring[j, 1]
        for copy in lines(j):
            copy.start()

    def do_piece(j):
        for copy in lines(j):
            copy.wait_recv()
        piece[j] = acc[j, :, :, me.yz] + line[j, 0] + line[j, 1] + line[j, 2]

    load_windows(0)

    @pl.loop(0, layers - 1)
    def _(layer):
        load_windows(layer + 1)
        field_factor = (medium[0], medium[1])
        blocks = [times(window_of(layer, p), wave_of(layer, p)) for p in range(count)]
        blocks = [times(b, field_factor) for b in forward(blocks)]
        for p, block in enumerate(inverse(blocks)):
            waves[layer + 1, p, 0] = block[0]
            waves[layer + 1, p, 1] = block[1]

    last = layers - 1
    blocks = [times(window_of(last, p), wave_of(last, p)) for p in range(count)]
    scaled = []
    for p, block in enumerate(forward(blocks)):
        miss = (2.0 * factor) * (block[0] * block[0] + block[1] * block[1] - measured_ref[p])
        scaled.append((miss * block[0], miss * block[1]))
    for p, block in enumerate(inverse(scaled)):
        pend[0, p, 0] = block[0]
        pend[0, p, 1] = block[1]

    @pl.loop(0, layers - 1)
    def _(i):
        @pl.when(i >= 6)
        def _():
            do_line(i - 6)

        @pl.when(i >= 4)
        def _():
            do_ring(i - 4)

        @pl.when(i >= 2)
        def _():
            do_fold(i - 2)

        @pl.when(i >= 1)
        def _():
            do_share(i - 1)

        slot = lax.rem(i, 2)
        layer = layers - 2 - i
        field_factor = (medium[0], medium[1])
        blocks = [conj_times(window_of(layer + 1, p), (pend[slot, p, 0], pend[slot, p, 1])) for p in range(count)]
        blocks = [conj_times(field_factor, b) for b in forward(blocks)]
        blocks = inverse(blocks)
        add_grads(i, slot)
        for p, block in enumerate(blocks):
            pend[1 - slot, p, 0] = block[0]
            pend[1 - slot, p, 1] = block[1]

    do_share(6)
    add_grads(7, 1)
    do_share(7)
    do_fold(5)
    do_ring(3)
    do_line(1)
    do_fold(6)
    do_ring(4)
    do_line(2)
    do_fold(7)
    do_ring(5)
    do_line(3)
    do_piece(0)
    do_ring(6)
    do_line(4)
    do_piece(1)
    do_ring(7)
    do_line(5)
    do_piece(2)
    do_line(6)
    do_piece(3)
    do_line(7)
    for j in range(4, 8):
        do_piece(j)

    for s in range(layers):
        inverse_index = jnp.zeros((), jnp.int32)
        for k in range(layers):
            inverse_index = jnp.where(order_ref[k] == s, layers - 1 - k, inverse_index)
        stage[s] = piece[inverse_index]
    to_x = [remote(stage.at[pl.ds(ZH * me.xs(d), ZH)], xbox.at[d - 1], end_send.at[d - 1], end_recv.at[d - 1],
                   me.device(x=me.xs(d))) for d in range(1, X)]
    for copy in to_x:
        copy.start()
    for copy in to_x:
        copy.wait_recv()
    pair[...] = stage[pl.ds(ZH * x, ZH)] + xbox[0] + xbox[1] + xbox[2]
    to_z = remote(pair.at[1 - me.zh], zbox, end_send.at[3], end_recv.at[3], me.device(z=me.zs(4)))
    to_z.start()
    to_z.wait_recv()
    total = pair[me.zh] + zbox[...]
    for half in range(2):
        for part in range(2):
            final[half, pl.ds(part, 8, stride=2), :] = total[half, part]
        out_ref[:, half * lanes:(half + 1) * lanes] = final[half]

    net.drain()
    for j in range(layers):
        for copy in [share(j)] + [f(j, side) for f in (hop_of, ring_of) for side in range(2)] + lines(j):
            copy.wait_send()
    for copy in to_x + [to_z]:
        copy.wait_send()


def per_device(object_slices, probe_wave, propagator_phase, measured, offsets, slice_order):
    layers = slice_order.shape[0]
    width = object_slices.shape[3]
    length = probe_wave.shape[1]
    count = offsets.shape[0]
    positions_total = count * lax.axis_size("depth") * lax.axis_size("pos")
    factor = 0.25 * width / (length * math.sqrt(positions_total))
    table = jnp.asarray(dft_tables(length))
    vmem = pl.BlockSpec(memory_space=pltpu.VMEM)
    smem = pl.BlockSpec(memory_space=pltpu.SMEM)
    anywhere = pl.BlockSpec(memory_space=pl.ANY)
    dma = pltpu.SemaphoreType.DMA
    block = (2, 2, 8, 128)
    total = pl.pallas_call(
        functools.partial(kernel, factor),
        out_shape=jax.ShapeDtypeStruct((16, width), F32),
        in_specs=[smem, smem, vmem] + [anywhere] * 4,
        out_specs=vmem,
        scratch_shapes=[
            pltpu.VMEM((2, layers, Y * ZL, 2, 16, 128), BF16),
            pltpu.VMEM((2, length, length), F32),
            pltpu.VMEM((length, length), F32),
            pltpu.VMEM((count, length, length), F32),
            pltpu.VMEM((2, 2, 2 * length, 2 * length), BF16),
            pltpu.VMEM((2, length, length), F32),
            pltpu.VMEM((2, 2 * width, 128), F32),
            pltpu.VMEM((layers, count, 2, length, length), F32),
            pltpu.VMEM((layers, count, 2, length, length), F32),
            pltpu.VMEM((2, count, 2, length, length), F32),
            pltpu.VMEM((width, count * length), BF16),
            pltpu.VMEM((layers, 2, 2, Y * ZL, 2, 8, 128), F32),
            pltpu.VMEM((layers, 2, 2, Y * ZL, 8, 128), F32),
            pltpu.VMEM((layers, 2, 2, Y * ZL, 8, 128), F32),
            pltpu.VMEM((layers, 2, 2, ZL, 8, 128), F32),
            pltpu.VMEM((layers, 2, 2, 2, ZL, 8, 128), F32),
            pltpu.VMEM((layers, 3) + block, F32),
            pltpu.VMEM((layers,) + block, F32),
            pltpu.VMEM((layers,) + block, F32),
            pltpu.VMEM((3, 2) + block, F32),
            pltpu.VMEM((2,) + block, F32),
            pltpu.VMEM(block, F32),
            pltpu.VMEM((2, 16, 128), F32),
            dma((4,)), dma((GATHER_COPIES,)), dma((GATHER_COPIES,)),
            dma((layers,)), dma((layers,)),
            dma((layers, 2)), dma((layers, 2)), dma((layers, 2)), dma((layers, 2)),
            dma((layers, 3)), dma((layers, 3)), dma((4,)), dma((4,)),
        ],
        compiler_params=pltpu.CompilerParams(collective_id=0, has_side_effects=True, vmem_limit_bytes=56 * 2**20),
    )(offsets, slice_order, object_slices.reshape(16, width), probe_wave, propagator_phase, measured, table)
    return total.reshape(object_slices.shape)


def solution(mesh):
    in_specs = (
        P("depth", "pos", None, None),
        P(),
        P(),
        P(("depth", "pos"), None, None),
        P(("depth", "pos"), None),
        P(),
    )
    out_specs = P("depth", "pos", None, None)
    return jax.shard_map(
        per_device, mesh=mesh, in_specs=in_specs, out_specs=out_specs, check_vma=False
    )
```

```python
import functools
import math

import jax
import jax.numpy as jnp
import ml_dtypes
import numpy as np
from jax import lax
from jax.experimental import pallas as pl
from jax.experimental.pallas import tpu as pltpu
from jax.sharding import PartitionSpec as P

BF16 = jnp.bfloat16
F32 = jnp.float32
X, ZH, Y, ZL = 4, 2, 4, 4
Z = ZH * ZL
MESH = pl.DeviceIdType.MESH
RING, LINE = 5, 7


def dft_tables(length):
    index = np.arange(length)
    angle = -2.0 * np.pi / length * ((index[:, None] * index[None, :]) % length)
    real, imag = np.cos(angle) / math.sqrt(length), np.sin(angle) / math.sqrt(length)
    full = np.block([[real, imag], [-imag, real]])
    pairs = []
    for matrix in (full, full.T):
        high = matrix.astype(ml_dtypes.bfloat16)
        low = (matrix - high.astype(np.float64)).astype(ml_dtypes.bfloat16)
        pairs.append(np.stack([high, low]))
    return np.stack(pairs)


class Place:
    def __init__(self):
        depth, pos = lax.axis_index("depth"), lax.axis_index("pos")
        self.depth = depth
        self.x, self.zh = depth // ZH, depth % ZH
        self.core = pos % 2
        self.yz = pos // 2
        self.y, self.zl = self.yz // ZL, self.yz % ZL
        self.z = self.zh * ZL + self.zl

    def device(self, x=None, y=None, z=None, core=None):
        x = self.x if x is None else x
        y = self.y if y is None else y
        z = self.z if z is None else z
        core = self.core if core is None else core
        return (x * ZH + z // ZL, (y * ZL + z % ZL) * 2 + core)

    def xs(self, d):
        return (self.x + d) % X

    def ys(self, d):
        return (self.y + d) % Y

    def zs(self, d):
        return (self.z + d) % Z


def greet(me):
    barrier = pltpu.get_barrier_semaphore()
    partners = [me.device(core=1 - me.core)]
    partners += [me.device(x=me.xs(d)) for d in range(1, X)]
    partners += [me.device(y=me.ys(d)) for d in range(1, Y)]
    partners += [me.device(z=me.zs(d)) for d in range(1, Z)]
    for device in partners:
        pl.semaphore_signal(barrier, inc=1, device_id=device, device_id_type=MESH)
    pl.semaphore_wait(barrier, len(partners))


def settle(ref, sem):
    pltpu.make_async_copy(ref, ref, sem).wait()


def remote(src, dst, send_sem, recv_sem, device):
    return pltpu.make_async_remote_copy(
        src_ref=src, dst_ref=dst, send_sem=send_sem, recv_sem=recv_sem, device_id=device, device_id_type=MESH)


def gather_whole(me, out, send, recv, meanwhile):
    x, y, c = me.x, me.y, me.core

    def push(spot, send_sem, recv_sem, device):
        remote(out.at[spot], out.at[spot], send.at[send_sem], recv.at[recv_sem], device).start()

    own = (slice(None), me.depth, me.yz, c)
    for d in (4, 3, 5, 2, 6, 1, 7):
        push(own, 0, 0, me.device(z=me.zs(d)))
    meanwhile()
    seven = out.at[:, pl.ds(0, 1), pl.ds(0, 7), 0]
    settle(seven, recv.at[0])

    first = (me.xs, me.ys)
    second = (me.ys, me.xs)
    to_first = (lambda d: me.device(x=me.xs(d)), lambda d: me.device(y=me.ys(d)))
    to_second = (lambda d: me.device(y=me.ys(d)), lambda d: me.device(x=me.xs(d)))

    def line(half):
        return (half, pl.ds(ZH * x, ZH), pl.ds(ZL * y, ZL), c)

    def unit(half, second):
        if half == 0:
            return (0, slice(None), pl.ds(ZL * second, ZL), c)
        return (1, pl.ds(ZH * second, ZH), slice(None), c)

    three_lines = out.at[0, pl.ds(0, 3), pl.ds(0, 8), 0]
    three_units = out.at[0, pl.ds(0, 6), :, 0]
    for d in (2, 1, 3):
        for half in range(2):
            push(line(half), 1 + half, 1 + half, to_first[half](d))
    for half in range(2):
        settle(three_lines, recv.at[1 + half])
        for d in (2, 1, 3):
            push(unit(half, second[half](0)), 3 + half, 4 + 3 * half + d, to_second[half](d))
    for half in range(2):
        push(unit(half, second[half](0)), 5 + half, 3 + half * 8, me.device(core=1 - c))
    for d in (1, 3, 2):
        for half in range(2):
            spot = unit(half, second[half](4 - d))
            settle(out.at[spot], recv.at[4 + 3 * half + d])
            push(spot, 5 + half, 3 + half * 8, me.device(core=1 - c))
    for half in range(2):
        settle(out.at[half, :, :, 1 - c], recv.at[3 + half * 8])

    def drain():
        settle(seven, send.at[0])
        for half in range(2):
            settle(three_lines, send.at[1 + half])
            settle(three_units, send.at[3 + half])
            settle(out.at[half, :, :, c], send.at[5 + half])

    return drain


def split(value):
    high = value.astype(BF16)
    return high, (value - high.astype(F32)).astype(BF16)


def dot(left, right):
    return jnp.dot(left, right, preferred_element_type=F32)


def times(a, b):
    return (a[0] * b[0] - a[1] * b[1], a[0] * b[1] + a[1] * b[0])


def conj_times(a, b):
    return (a[0] * b[0] + a[1] * b[1], a[0] * b[1] - a[1] * b[0])


def kernel(factor, offsets_ref, order_ref, block_ref, probe_hbm, phase_hbm, measured_hbm, table_hbm, out_ref,
           whole, probe_ref, phase_ref, measured_ref, table_ref, medium, slab, windows, waves, pend, place_ref,
           grads, inbox, acc, hop, ring, line, piece, stage, xbox, pair, zbox, final,
           load_sem, send, recv, s1_send, s1_recv, hop_send, hop_recv, ring_send, ring_recv, line_send, line_recv,
           end_send, end_recv):
    layers = order_ref.shape[0]
    count, length = measured_ref.shape[:2]
    lanes = whole.shape[-1]
    field = 2 * lanes
    me = Place()
    x, y, c = me.x, me.y, me.core
    other = 1 - c
    loads = [
        pltpu.make_async_copy(src, dst, load_sem.at[i])
        for i, (src, dst) in enumerate((
            (phase_hbm, phase_ref), (probe_hbm, probe_ref), (table_hbm, table_ref), (measured_hbm, measured_ref)))
    ]
    for load in loads:
        load.start()
    for row in range(block_ref.shape[1]):
        for half in range(2):
            whole[half, me.depth, me.yz, c, 2 * row:2 * row + 2] = block_ref[0, row, :, half * lanes:(half + 1) * lanes]
    greet(me)
    lane = lax.broadcasted_iota(jnp.int32, (length, lanes), 1)

    def prepare():
        for load in loads:
            load.wait()
        medium[0] = jnp.cos(phase_ref[...])
        medium[1] = jnp.sin(phase_ref[...])
        rows = lax.broadcasted_iota(jnp.int32, (field, length), 0)
        inner = lax.broadcasted_iota(jnp.int32, (field, length), 1)
        for p in range(count):
            hit = rows - inner == offsets_ref[0, p]
            place_ref[:, p * length:(p + 1) * length] = jnp.where(hit, 1.0, 0.0).astype(BF16)
            waves[0, p] = probe_ref[...]

    drain_gather = gather_whole(me, whole, send, recv, prepare)

    def right_map(blocks, which):
        high_table, low_table = table_ref[which, 0], table_ref[which, 1]
        results = []
        for block in blocks:
            high, low = split(jnp.concatenate(block, axis=1))
            out = dot(high, high_table) + (dot(low, high_table) + dot(high, low_table))
            results.append((out[:, :length], out[:, length:]))
        return results

    def left_map(blocks, which):
        high_table, low_table = table_ref[which, 0], table_ref[which, 1]
        stacked = jnp.concatenate([jnp.concatenate(block, axis=0) for block in blocks], axis=1)
        high, low = split(stacked)
        out = dot(high_table, high) + (dot(high_table, low) + dot(low_table, high))
        return [
            (out[:length, i * length:(i + 1) * length], out[length:, i * length:(i + 1) * length])
            for i in range(len(blocks))
        ]

    def forward(blocks):
        return left_map(right_map(blocks, 0), 1)

    def inverse(blocks):
        return left_map(right_map(blocks, 1), 0)

    def load_windows(layer):
        index = order_ref[layer]
        for half in range(2):
            slab[half] = whole[half, index].reshape(2 * field, lanes).astype(F32)
        for p in range(count):
            row, column = offsets_ref[0, p], offsets_ref[1, p]
            shift = lax.rem(lanes - column, lanes)
            keep = lane < lanes - column
            for part in range(2):
                left = slab[0, pl.ds(2 * row + part, length, stride=2), :]
                right = slab[1, pl.ds(2 * row + part, length, stride=2), :]
                windows[layer, p, part] = jnp.where(keep, pltpu.roll(left, shift, 1), pltpu.roll(right, shift, 1))

    def window_of(layer, p):
        return windows[layer, p, 0], windows[layer, p, 1]

    def wave_of(layer, p):
        return waves[layer, p, 0], waves[layer, p, 1]

    def add_grads(j, slot):
        layer = layers - 1 - j
        terms = [conj_times(wave_of(layer, p), (pend[slot, p, 0], pend[slot, p, 1])) for p in range(count)]
        for part in range(2):
            moved = []
            for p in range(count):
                column = offsets_ref[1, p]
                turned = pltpu.roll(terms[p][part], lax.rem(column, lanes), 1)
                moved.append(jnp.concatenate(
                    [jnp.where(lane >= column, turned, 0.0), jnp.where(lane >= column, 0.0, turned)], axis=1))
            high, low = split(jnp.concatenate(moved, axis=0))
            total = dot(place_ref[...], high) + dot(place_ref[...], low)
            for half in range(2):
                grads[j, half, part] = total[:, half * lanes:(half + 1) * lanes].reshape(Y * ZL, 2, 8, lanes)

    def y_unit(d):
        return pl.ds(ZL * me.ys(d), ZL)

    def do_share(j):
        remote(grads.at[j, :, :, :, other], inbox.at[j], s1_send.at[0], s1_recv.at[j], me.device(core=other)).start()

    def do_fold(j):
        settle(inbox.at[j], s1_recv.at[j])
        acc[j] = grads[j, :, :, :, c] + inbox[j]
        for side in range(2):
            remote(acc.at[j, side, :, y_unit(2)], hop.at[j, side], hop_send.at[0], hop_recv.at[j, side],
                   me.device(y=me.ys(1 + 2 * side))).start()

    def do_ring(j):
        for side in range(2):
            unit = y_unit(1 + 2 * side)
            settle(hop.at[j, side], hop_recv.at[j, side])
            acc[j, side, :, unit] = acc[j, side, :, unit] + hop[j, side]
            remote(acc.at[j, :, :, unit], ring.at[j, side], ring_send.at[0], ring_recv.at[j, side],
                   me.device(y=me.ys(1 + 2 * side))).start()

    def do_line(j):
        for side in range(2):
            settle(ring.at[j, side], ring_recv.at[j, side])
        acc[j, :, :, y_unit(0)] = acc[j, :, :, y_unit(0)] + ring[j, 0] + ring[j, 1]
        for d in (2, 3, 1):
            zl = (me.zl + d) % ZL
            remote(acc.at[j, :, :, ZL * y + zl], line.at[j, d - 1], line_send.at[0], line_recv.at[j],
                   me.device(z=me.zh * ZL + zl)).start()

    def do_piece(j):
        settle(line.at[j], line_recv.at[j])
        piece[j] = acc[j, :, :, me.yz] + line[j, 0] + line[j, 1] + line[j, 2]

    load_windows(0)

    @pl.loop(0, layers - 1)
    def _(layer):
        load_windows(layer + 1)
        field_factor = (medium[0], medium[1])
        blocks = [times(window_of(layer, p), wave_of(layer, p)) for p in range(count)]
        blocks = [times(b, field_factor) for b in forward(blocks)]
        for p, block in enumerate(inverse(blocks)):
            waves[layer + 1, p, 0] = block[0]
            waves[layer + 1, p, 1] = block[1]

    last = layers - 1
    blocks = [times(window_of(last, p), wave_of(last, p)) for p in range(count)]
    scaled = []
    for p, block in enumerate(forward(blocks)):
        miss = (2.0 * factor) * (block[0] * block[0] + block[1] * block[1] - measured_ref[p])
        scaled.append((miss * block[0], miss * block[1]))
    for p, block in enumerate(inverse(scaled)):
        pend[0, p, 0] = block[0]
        pend[0, p, 1] = block[1]

    @pl.loop(0, layers - 1)
    def _(i):
        @pl.when(i >= LINE)
        def _():
            do_line(i - LINE)

        @pl.when(i >= RING)
        def _():
            do_ring(i - RING)

        @pl.when(i >= 3)
        def _():
            do_fold(i - 3)

        @pl.when(i >= 1)
        def _():
            do_share(i - 1)

        slot = lax.rem(i, 2)
        layer = layers - 2 - i
        field_factor = (medium[0], medium[1])
        blocks = [conj_times(window_of(layer + 1, p), (pend[slot, p, 0], pend[slot, p, 1])) for p in range(count)]
        blocks = [conj_times(field_factor, b) for b in forward(blocks)]
        blocks = inverse(blocks)
        add_grads(i, slot)
        for p, block in enumerate(blocks):
            pend[1 - slot, p, 0] = block[0]
            pend[1 - slot, p, 1] = block[1]

    do_share(6)
    add_grads(7, 1)
    do_share(7)
    do_fold(4)
    do_fold(5)
    for j in range(7 - RING, 4):
        do_ring(j)
    do_fold(6)
    drain_gather()
    do_fold(7)
    do_ring(4)
    do_ring(5)
    for j in range(7 - LINE, 3):
        do_line(j)
    do_ring(6)
    do_line(3)
    do_line(4)
    do_ring(7)
    do_line(5)
    do_line(6)
    for j in range(5):
        do_piece(j)
    do_line(7)
    for j in range(5, 8):
        do_piece(j)

    for s in range(layers):
        inverse_index = jnp.zeros((), jnp.int32)
        for k in range(layers):
            inverse_index = jnp.where(order_ref[k] == s, layers - 1 - k, inverse_index)
        stage[s] = piece[inverse_index]
    for d in (2, 1, 3):
        remote(stage.at[pl.ds(ZH * me.xs(d), ZH)], xbox.at[d - 1], end_send.at[0], end_recv.at[0],
               me.device(x=me.xs(d))).start()
    settle(inbox, s1_send.at[0])
    settle(hop, hop_send.at[0])
    settle(xbox, end_recv.at[0])
    pair[...] = stage[pl.ds(ZH * x, ZH)] + xbox[0] + xbox[1] + xbox[2]
    to_z = remote(pair.at[1 - me.zh], zbox, end_send.at[1], end_recv.at[1], me.device(z=me.zs(4)))
    to_z.start()
    settle(ring, ring_send.at[0])
    settle(line, line_send.at[0])
    settle(xbox, end_send.at[0])
    to_z.wait()
    total = pair[me.zh] + zbox[...]
    for half in range(2):
        for part in range(2):
            final[half, pl.ds(part, 8, stride=2), :] = total[half, part]
        out_ref[:, half * lanes:(half + 1) * lanes] = final[half]


def per_device(object_slices, probe_wave, propagator_phase, measured, offsets, slice_order):
    layers = slice_order.shape[0]
    width = object_slices.shape[3]
    length = probe_wave.shape[1]
    count = offsets.shape[0]
    positions_total = count * lax.axis_size("depth") * lax.axis_size("pos")
    factor = 0.25 * width / (length * math.sqrt(positions_total))
    table = jnp.asarray(dft_tables(length))
    vmem = pl.BlockSpec(memory_space=pltpu.VMEM)
    smem = pl.BlockSpec(memory_space=pltpu.SMEM)
    anywhere = pl.BlockSpec(memory_space=pl.ANY)
    dma = pltpu.SemaphoreType.DMA
    block = (2, 2, 8, 128)
    total = pl.pallas_call(
        functools.partial(kernel, factor),
        out_shape=jax.ShapeDtypeStruct((16, width), F32),
        in_specs=[smem, smem, vmem] + [anywhere] * 4,
        out_specs=vmem,
        scratch_shapes=[
            pltpu.VMEM((2, layers, Y * ZL, 2, 16, 128), BF16),
            pltpu.VMEM((2, length, length), F32),
            pltpu.VMEM((length, length), F32),
            pltpu.VMEM((count, length, length), F32),
            pltpu.VMEM((2, 2, 2 * length, 2 * length), BF16),
            pltpu.VMEM((2, length, length), F32),
            pltpu.VMEM((2, 2 * width, 128), F32),
            pltpu.VMEM((layers, count, 2, length, length), F32),
            pltpu.VMEM((layers, count, 2, length, length), F32),
            pltpu.VMEM((2, count, 2, length, length), F32),
            pltpu.VMEM((width, count * length), BF16),
            pltpu.VMEM((layers, 2, 2, Y * ZL, 2, 8, 128), F32),
            pltpu.VMEM((layers, 2, 2, Y * ZL, 8, 128), F32),
            pltpu.VMEM((layers, 2, 2, Y * ZL, 8, 128), F32),
            pltpu.VMEM((layers, 2, 2, ZL, 8, 128), F32),
            pltpu.VMEM((layers, 2, 2, 2, ZL, 8, 128), F32),
            pltpu.VMEM((layers, 3) + block, F32),
            pltpu.VMEM((layers,) + block, F32),
            pltpu.VMEM((layers,) + block, F32),
            pltpu.VMEM((3, 2) + block, F32),
            pltpu.VMEM((2,) + block, F32),
            pltpu.VMEM(block, F32),
            pltpu.VMEM((2, 16, 128), F32),
            dma((4,)), dma((7,)), dma((12,)),
            dma((1,)), dma((layers,)), dma((1,)), dma((layers, 2)), dma((1,)), dma((layers, 2)),
            dma((1,)), dma((layers,)), dma((2,)), dma((2,)),
        ],
        compiler_params=pltpu.CompilerParams(collective_id=0, has_side_effects=True, vmem_limit_bytes=56 * 2**20),
    )(offsets.T, slice_order, object_slices, probe_wave, propagator_phase, measured, table)
    return total.reshape(object_slices.shape)


def solution(mesh):
    in_specs = (
        P("depth", "pos", None, None),
        P(),
        P(),
        P(("depth", "pos"), None, None),
        P(("depth", "pos"), None),
        P(),
    )
    out_specs = P("depth", "pos", None, None)
    return jax.shard_map(
        per_device, mesh=mesh, in_specs=in_specs, out_specs=out_specs, check_vma=False
    )
```

```python
import functools
import math

import jax
import jax.numpy as jnp
import ml_dtypes
import numpy as np
from jax import lax
from jax.experimental import pallas as pl
from jax.experimental.pallas import tpu as pltpu
from jax.sharding import PartitionSpec as P

BF16 = jnp.bfloat16
F32 = jnp.float32
X, ZH, Y, ZL = 4, 2, 4, 4
Z = ZH * ZL
MESH = pl.DeviceIdType.MESH
RING, LINE = 5, 7


def dft_tables(length):
    index = np.arange(length)
    angle = -2.0 * np.pi / length * ((index[:, None] * index[None, :]) % length)
    real, imag = np.cos(angle) / math.sqrt(length), np.sin(angle) / math.sqrt(length)
    full = np.block([[real, imag], [-imag, real]])
    pairs = []
    for matrix in (full, full.T):
        high = matrix.astype(ml_dtypes.bfloat16)
        low = (matrix - high.astype(np.float64)).astype(ml_dtypes.bfloat16)
        pairs.append(np.stack([high, low]))
    return np.stack(pairs)


class Place:
    def __init__(self):
        depth, pos = lax.axis_index("depth"), lax.axis_index("pos")
        self.depth = depth
        self.x, self.zh = depth // ZH, depth % ZH
        self.core = pos % 2
        self.yz = pos // 2
        self.y, self.zl = self.yz // ZL, self.yz % ZL
        self.z = self.zh * ZL + self.zl

    def device(self, x=None, y=None, z=None, core=None):
        x = self.x if x is None else x
        y = self.y if y is None else y
        z = self.z if z is None else z
        core = self.core if core is None else core
        return (x * ZH + z // ZL, (y * ZL + z % ZL) * 2 + core)

    def xs(self, d):
        return (self.x + d) % X

    def ys(self, d):
        return (self.y + d) % Y

    def zs(self, d):
        return (self.z + d) % Z


def greet(me):
    barrier = pltpu.get_barrier_semaphore()
    partners = [me.device(core=1 - me.core)]
    partners += [me.device(x=me.xs(d)) for d in range(1, X)]
    partners += [me.device(y=me.ys(d)) for d in range(1, Y)]
    partners += [me.device(z=me.zs(d)) for d in range(1, Z)]
    for device in partners:
        pl.semaphore_signal(barrier, inc=1, device_id=device, device_id_type=MESH)
    pl.semaphore_wait(barrier, len(partners))


def settle(ref, sem):
    pltpu.make_async_copy(ref, ref, sem).wait()


def remote(src, dst, send_sem, recv_sem, device):
    return pltpu.make_async_remote_copy(
        src_ref=src, dst_ref=dst, send_sem=send_sem, recv_sem=recv_sem, device_id=device, device_id_type=MESH)


def gather_whole(me, out, send, recv, meanwhile):
    x, y, c = me.x, me.y, me.core

    def push(spot, send_sem, recv_sem, device):
        remote(out.at[spot], out.at[spot], send.at[send_sem], recv.at[recv_sem], device).start()

    own = (slice(None), me.depth, me.yz, c)
    for d in (4, 3, 5, 2, 6, 1, 7):
        push(own, 0, 0, me.device(z=me.zs(d)))
    meanwhile()
    seven = out.at[:, pl.ds(0, 1), pl.ds(0, 7), 0]
    settle(seven, recv.at[0])

    first = (me.xs, me.ys)
    second = (me.ys, me.xs)
    to_first = (lambda d: me.device(x=me.xs(d)), lambda d: me.device(y=me.ys(d)))
    to_second = (lambda d: me.device(y=me.ys(d)), lambda d: me.device(x=me.xs(d)))

    def line(half):
        return (half, pl.ds(ZH * x, ZH), pl.ds(ZL * y, ZL), c)

    def unit(half, second):
        if half == 0:
            return (0, slice(None), pl.ds(ZL * second, ZL), c)
        return (1, pl.ds(ZH * second, ZH), slice(None), c)

    three_lines = out.at[0, pl.ds(0, 3), pl.ds(0, 8), 0]
    three_units = out.at[0, pl.ds(0, 6), :, 0]
    for d in (2, 1, 3):
        for half in range(2):
            push(line(half), 1 + half, 1 + half, to_first[half](d))
    for half in range(2):
        settle(three_lines, recv.at[1 + half])
        for d in (2, 1, 3):
            push(unit(half, second[half](0)), 3 + half, 4 + 3 * half + d, to_second[half](d))
    for half in range(2):
        push(unit(half, second[half](0)), 5 + half, 3 + half * 8, me.device(core=1 - c))
    for d in (1, 3, 2):
        for half in range(2):
            spot = unit(half, second[half](4 - d))
            settle(out.at[spot], recv.at[4 + 3 * half + d])
            push(spot, 5 + half, 3 + half * 8, me.device(core=1 - c))
    for half in range(2):
        settle(out.at[half, :, :, 1 - c], recv.at[3 + half * 8])

    def drain():
        settle(seven, send.at[0])
        for half in range(2):
            settle(three_lines, send.at[1 + half])
            settle(three_units, send.at[3 + half])
            settle(out.at[half, :, :, c], send.at[5 + half])

    return drain


def split(value):
    high = value.astype(BF16)
    return high, (value - high.astype(F32)).astype(BF16)


def dot(left, right):
    return jnp.dot(left, right, preferred_element_type=F32)


def times(a, b):
    return (a[0] * b[0] - a[1] * b[1], a[0] * b[1] + a[1] * b[0])


def conj_times(a, b):
    return (a[0] * b[0] + a[1] * b[1], a[0] * b[1] - a[1] * b[0])


def kernel(factor, offsets_ref, order_ref, block_ref, probe_hbm, phase_hbm, measured_hbm, table_hbm, out_ref,
           whole, probe_ref, phase_ref, measured_ref, table_ref, medium, slab, windows, waves, pend, place_ref,
           grads, inbox, acc, hop, ring, line, piece, stage, xbox, pair, zbox, final,
           load_sem, send, recv, s1_send, s1_recv, hop_send, hop_recv, ring_send, ring_recv, line_send, line_recv,
           end_send, end_recv):
    layers = order_ref.shape[0]
    count, length = measured_ref.shape[:2]
    lanes = whole.shape[-1]
    field = 2 * lanes
    me = Place()
    x, y, c = me.x, me.y, me.core
    other = 1 - c
    loads = [
        pltpu.make_async_copy(src, dst, load_sem.at[i])
        for i, (src, dst) in enumerate((
            (phase_hbm, phase_ref), (probe_hbm, probe_ref), (table_hbm, table_ref), (measured_hbm, measured_ref)))
    ]
    for load in loads:
        load.start()
    for row in range(block_ref.shape[1]):
        for half in range(2):
            whole[half, me.depth, me.yz, c, 2 * row:2 * row + 2] = block_ref[0, row, :, half * lanes:(half + 1) * lanes]
    greet(me)
    lane = lax.broadcasted_iota(jnp.int32, (length, lanes), 1)

    def prepare():
        for load in loads:
            load.wait()
        medium[0] = jnp.cos(phase_ref[...])
        medium[1] = jnp.sin(phase_ref[...])
        rows = lax.broadcasted_iota(jnp.int32, (field, length), 0)
        inner = lax.broadcasted_iota(jnp.int32, (field, length), 1)
        for p in range(count):
            hit = rows - inner == offsets_ref[0, p]
            place_ref[:, p * length:(p + 1) * length] = jnp.where(hit, 1.0, 0.0).astype(BF16)
            waves[0, p] = probe_ref[...]

    drain_gather = gather_whole(me, whole, send, recv, prepare)

    def right_map(blocks, which):
        high_table, low_table = table_ref[which, 0], table_ref[which, 1]
        results = []
        for block in blocks:
            high, low = split(jnp.concatenate(block, axis=1))
            out = dot(high, high_table) + (dot(low, high_table) + dot(high, low_table))
            results.append((out[:, :length], out[:, length:]))
        return results

    def left_map(blocks, which):
        high_table, low_table = table_ref[which, 0], table_ref[which, 1]
        stacked = jnp.concatenate([jnp.concatenate(block, axis=0) for block in blocks], axis=1)
        high, low = split(stacked)
        out = dot(high_table, high) + (dot(high_table, low) + dot(low_table, high))
        return [
            (out[:length, i * length:(i + 1) * length], out[length:, i * length:(i + 1) * length])
            for i in range(len(blocks))
        ]

    def forward(blocks):
        return left_map(right_map(blocks, 0), 1)

    def inverse(blocks):
        return left_map(right_map(blocks, 1), 0)

    def load_windows(layer):
        index = order_ref[layer]
        for half in range(2):
            slab[half] = whole[half, index].reshape(2 * field, lanes).astype(F32)
        for p in range(count):
            row, column = offsets_ref[0, p], offsets_ref[1, p]
            shift = lax.rem(lanes - column, lanes)
            keep = lane < lanes - column
            for part in range(2):
                left = slab[0, pl.ds(2 * row + part, length, stride=2), :]
                right = slab[1, pl.ds(2 * row + part, length, stride=2), :]
                windows[layer, p, part] = jnp.where(keep, pltpu.roll(left, shift, 1), pltpu.roll(right, shift, 1))

    def window_of(layer, p):
        return windows[layer, p, 0], windows[layer, p, 1]

    def wave_of(layer, p):
        return waves[layer, p, 0], waves[layer, p, 1]

    def add_grads(j, slot):
        layer = layers - 1 - j
        terms = [conj_times(wave_of(layer, p), (pend[slot, p, 0], pend[slot, p, 1])) for p in range(count)]
        for part in range(2):
            moved = []
            for p in range(count):
                column = offsets_ref[1, p]
                turned = pltpu.roll(terms[p][part], lax.rem(column, lanes), 1)
                moved.append(jnp.concatenate(
                    [jnp.where(lane >= column, turned, 0.0), jnp.where(lane >= column, 0.0, turned)], axis=1))
            high, low = split(jnp.concatenate(moved, axis=0))
            total = dot(place_ref[...], high) + dot(place_ref[...], low)
            for half in range(2):
                grads[j, half, part] = total[:, half * lanes:(half + 1) * lanes].reshape(Y * ZL, 2, 8, lanes)

    def y_unit(d):
        return pl.ds(ZL * me.ys(d), ZL)

    def do_share(j):
        remote(grads.at[j, :, :, :, other], inbox.at[j], s1_send.at[0], s1_recv.at[j], me.device(core=other)).start()

    def do_fold(j):
        settle(inbox.at[j], s1_recv.at[j])
        acc[j] = grads[j, :, :, :, c] + inbox[j]
        for side in range(2):
            remote(acc.at[j, side, :, y_unit(2)], hop.at[j, side], hop_send.at[0], hop_recv.at[j, side],
                   me.device(y=me.ys(1 + 2 * side))).start()

    def do_ring(j):
        for side in range(2):
            unit = y_unit(1 + 2 * side)
            settle(hop.at[j, side], hop_recv.at[j, side])
            acc[j, side, :, unit] = acc[j, side, :, unit] + hop[j, side]
            remote(acc.at[j, :, :, unit], ring.at[j, side], ring_send.at[0], ring_recv.at[j, side],
                   me.device(y=me.ys(1 + 2 * side))).start()

    def do_line(j):
        for side in range(2):
            settle(ring.at[j, side], ring_recv.at[j, side])
        acc[j, :, :, y_unit(0)] = acc[j, :, :, y_unit(0)] + ring[j, 0] + ring[j, 1]
        for d in (2, 3, 1):
            zl = (me.zl + d) % ZL
            remote(acc.at[j, :, :, ZL * y + zl], line.at[j, d - 1], line_send.at[0], line_recv.at[j],
                   me.device(z=me.zh * ZL + zl)).start()

    def do_piece(j):
        settle(line.at[j], line_recv.at[j])
        piece[j] = acc[j, :, :, me.yz] + line[j, 0] + line[j, 1] + line[j, 2]

    load_windows(0)

    @pl.loop(0, layers - 1, unroll=7)
    def _(layer):
        load_windows(layer + 1)
        field_factor = (medium[0], medium[1])
        blocks = [times(window_of(layer, p), wave_of(layer, p)) for p in range(count)]
        blocks = [times(b, field_factor) for b in forward(blocks)]
        for p, block in enumerate(inverse(blocks)):
            waves[layer + 1, p, 0] = block[0]
            waves[layer + 1, p, 1] = block[1]

    last = layers - 1
    blocks = [times(window_of(last, p), wave_of(last, p)) for p in range(count)]
    scaled = []
    for p, block in enumerate(forward(blocks)):
        miss = (2.0 * factor) * (block[0] * block[0] + block[1] * block[1] - measured_ref[p])
        scaled.append((miss * block[0], miss * block[1]))
    for p, block in enumerate(inverse(scaled)):
        pend[0, p, 0] = block[0]
        pend[0, p, 1] = block[1]

    @pl.loop(0, layers - 1)
    def _(i):
        @pl.when(i >= LINE)
        def _():
            do_line(i - LINE)

        @pl.when(i >= RING)
        def _():
            do_ring(i - RING)

        @pl.when(i >= 3)
        def _():
            do_fold(i - 3)

        @pl.when(i >= 1)
        def _():
            do_share(i - 1)

        slot = lax.rem(i, 2)
        layer = layers - 2 - i
        field_factor = (medium[0], medium[1])
        blocks = [conj_times(window_of(layer + 1, p), (pend[slot, p, 0], pend[slot, p, 1])) for p in range(count)]
        blocks = [conj_times(field_factor, b) for b in forward(blocks)]
        blocks = inverse(blocks)
        add_grads(i, slot)
        for p, block in enumerate(blocks):
            pend[1 - slot, p, 0] = block[0]
            pend[1 - slot, p, 1] = block[1]

    do_share(6)
    add_grads(7, 1)
    do_share(7)
    do_fold(4)
    do_fold(5)
    for j in range(7 - RING, 4):
        do_ring(j)
    do_fold(6)
    drain_gather()
    do_fold(7)
    do_ring(4)
    do_ring(5)
    for j in range(7 - LINE, 3):
        do_line(j)
    do_ring(6)
    do_line(3)
    do_line(4)
    do_ring(7)
    do_line(5)
    do_line(6)
    for j in range(5):
        do_piece(j)
    do_line(7)
    for j in range(5, 8):
        do_piece(j)

    for s in range(layers):
        inverse_index = jnp.zeros((), jnp.int32)
        for k in range(layers):
            inverse_index = jnp.where(order_ref[k] == s, layers - 1 - k, inverse_index)
        stage[s] = piece[inverse_index]
    for d in (2, 1, 3):
        remote(stage.at[pl.ds(ZH * me.xs(d), ZH)], xbox.at[d - 1], end_send.at[0], end_recv.at[0],
               me.device(x=me.xs(d))).start()
    settle(inbox, s1_send.at[0])
    settle(hop, hop_send.at[0])
    settle(xbox, end_recv.at[0])
    pair[...] = stage[pl.ds(ZH * x, ZH)] + xbox[0] + xbox[1] + xbox[2]
    to_z = remote(pair.at[1 - me.zh], zbox, end_send.at[1], end_recv.at[1], me.device(z=me.zs(4)))
    to_z.start()
    settle(ring, ring_send.at[0])
    settle(line, line_send.at[0])
    settle(xbox, end_send.at[0])
    to_z.wait()
    total = pair[me.zh] + zbox[...]
    for half in range(2):
        for part in range(2):
            final[half, pl.ds(part, 8, stride=2), :] = total[half, part]
        out_ref[:, half * lanes:(half + 1) * lanes] = final[half]


def per_device(object_slices, probe_wave, propagator_phase, measured, offsets, slice_order):
    layers = slice_order.shape[0]
    width = object_slices.shape[3]
    length = probe_wave.shape[1]
    count = offsets.shape[0]
    positions_total = count * lax.axis_size("depth") * lax.axis_size("pos")
    factor = 0.25 * width / (length * math.sqrt(positions_total))
    table = jnp.asarray(dft_tables(length))
    vmem = pl.BlockSpec(memory_space=pltpu.VMEM)
    smem = pl.BlockSpec(memory_space=pltpu.SMEM)
    anywhere = pl.BlockSpec(memory_space=pl.ANY)
    dma = pltpu.SemaphoreType.DMA
    block = (2, 2, 8, 128)
    total = pl.pallas_call(
        functools.partial(kernel, factor),
        out_shape=jax.ShapeDtypeStruct((16, width), F32),
        in_specs=[smem, smem, vmem] + [anywhere] * 4,
        out_specs=vmem,
        scratch_shapes=[
            pltpu.VMEM((2, layers, Y * ZL, 2, 16, 128), BF16),
            pltpu.VMEM((2, length, length), F32),
            pltpu.VMEM((length, length), F32),
            pltpu.VMEM((count, length, length), F32),
            pltpu.VMEM((2, 2, 2 * length, 2 * length), BF16),
            pltpu.VMEM((2, length, length), F32),
            pltpu.VMEM((2, 2 * width, 128), F32),
            pltpu.VMEM((layers, count, 2, length, length), F32),
            pltpu.VMEM((layers, count, 2, length, length), F32),
            pltpu.VMEM((2, count, 2, length, length), F32),
            pltpu.VMEM((width, count * length), BF16),
            pltpu.VMEM((layers, 2, 2, Y * ZL, 2, 8, 128), F32),
            pltpu.VMEM((layers, 2, 2, Y * ZL, 8, 128), F32),
            pltpu.VMEM((layers, 2, 2, Y * ZL, 8, 128), F32),
            pltpu.VMEM((layers, 2, 2, ZL, 8, 128), F32),
            pltpu.VMEM((layers, 2, 2, 2, ZL, 8, 128), F32),
            pltpu.VMEM((layers, 3) + block, F32),
            pltpu.VMEM((layers,) + block, F32),
            pltpu.VMEM((layers,) + block, F32),
            pltpu.VMEM((3, 2) + block, F32),
            pltpu.VMEM((2,) + block, F32),
            pltpu.VMEM(block, F32),
            pltpu.VMEM((2, 16, 128), F32),
            dma((4,)), dma((7,)), dma((12,)),
            dma((1,)), dma((layers,)), dma((1,)), dma((layers, 2)), dma((1,)), dma((layers, 2)),
            dma((1,)), dma((layers,)), dma((2,)), dma((2,)),
        ],
        compiler_params=pltpu.CompilerParams(collective_id=0, has_side_effects=True, vmem_limit_bytes=56 * 2**20),
    )(offsets.T, slice_order, object_slices, probe_wave, propagator_phase, measured, table)
    return total.reshape(object_slices.shape)


def solution(mesh):
    in_specs = (
        P("depth", "pos", None, None),
        P(),
        P(),
        P(("depth", "pos"), None, None),
        P(("depth", "pos"), None),
        P(),
    )
    out_specs = P("depth", "pos", None, None)
    return jax.shard_map(
        per_device, mesh=mesh, in_specs=in_specs, out_specs=out_specs, check_vma=False
    )
```

```python
import functools
import math

import jax
import jax.numpy as jnp
import ml_dtypes
import numpy as np
from jax import lax
from jax.experimental import pallas as pl
from jax.experimental.pallas import tpu as pltpu
from jax.sharding import PartitionSpec as P

BF16 = jnp.bfloat16
F32 = jnp.float32
X, ZH, Y, ZL = 4, 2, 4, 4
Z = ZH * ZL
MESH = pl.DeviceIdType.MESH
DEPTH_STEPS = ((2, ZL), (1, ZL), (3, ZL), (0, ZL), (2, 0), (1, 0), (3, 0))
RING, LINE = 5, 7


def dft_tables(length):
    index = np.arange(length)
    angle = -2.0 * np.pi / length * ((index[:, None] * index[None, :]) % length)
    real, imag = np.cos(angle) / math.sqrt(length), np.sin(angle) / math.sqrt(length)
    full = np.block([[real, imag], [-imag, real]])
    pairs = []
    for matrix in (full, full.T):
        high = matrix.astype(ml_dtypes.bfloat16)
        low = (matrix - high.astype(np.float64)).astype(ml_dtypes.bfloat16)
        pairs.append(np.stack([high, low]))
    return np.stack(pairs)


class Place:
    def __init__(self):
        depth, pos = lax.axis_index("depth"), lax.axis_index("pos")
        self.depth = depth
        self.x, self.zh = depth // ZH, depth % ZH
        self.core = pos % 2
        self.yz = pos // 2
        self.y, self.zl = self.yz // ZL, self.yz % ZL
        self.z = self.zh * ZL + self.zl

    def device(self, x=None, y=None, z=None, core=None):
        x = self.x if x is None else x
        y = self.y if y is None else y
        z = self.z if z is None else z
        core = self.core if core is None else core
        return (x * ZH + z // ZL, (y * ZL + z % ZL) * 2 + core)

    def xs(self, d):
        return (self.x + d) % X

    def ys(self, d):
        return (self.y + d) % Y

    def zs(self, d):
        return (self.z + d) % Z


def greet(me):
    barrier = pltpu.get_barrier_semaphore()
    partners = [me.device(core=1 - me.core)]
    partners += [me.device(x=me.xs(d)) for d in range(1, X)]
    partners += [me.device(y=me.ys(d)) for d in range(1, Y)]
    partners += [me.device(z=me.zs(d)) for d in range(1, Z)]
    partners += [me.device(x=me.xs(d), z=me.zs(ZL)) for d in range(1, X)]
    for device in partners:
        pl.semaphore_signal(barrier, inc=1, device_id=device, device_id_type=MESH)
    pl.semaphore_wait(barrier, len(partners))


def settle(ref, sem):
    pltpu.make_async_copy(ref, ref, sem).wait()


def remote(src, dst, send_sem, recv_sem, device):
    return pltpu.make_async_remote_copy(
        src_ref=src, dst_ref=dst, send_sem=send_sem, recv_sem=recv_sem, device_id=device, device_id_type=MESH)


def gather_whole(me, out, send, recv, meanwhile):
    x, y, c = me.x, me.y, me.core

    def push(spot, send_sem, recv_sem, device):
        remote(out.at[spot], out.at[spot], send.at[send_sem], recv.at[recv_sem], device).start()

    own = (slice(None), me.depth, me.yz, c)
    for d in (4, 3, 5, 2, 6, 1, 7):
        push(own, 0, 0, me.device(z=me.zs(d)))
    meanwhile()
    seven = out.at[:, pl.ds(0, 1), pl.ds(0, 7), 0]
    settle(seven, recv.at[0])

    first = (me.xs, me.ys)
    second = (me.ys, me.xs)
    to_first = (lambda d: me.device(x=me.xs(d)), lambda d: me.device(y=me.ys(d)))
    to_second = (lambda d: me.device(y=me.ys(d)), lambda d: me.device(x=me.xs(d)))

    def line(half):
        return (half, pl.ds(ZH * x, ZH), pl.ds(ZL * y, ZL), c)

    def unit(half, second):
        if half == 0:
            return (0, slice(None), pl.ds(ZL * second, ZL), c)
        return (1, pl.ds(ZH * second, ZH), slice(None), c)

    three_lines = out.at[0, pl.ds(0, 3), pl.ds(0, 8), 0]
    three_units = out.at[0, pl.ds(0, 6), :, 0]
    for d in (2, 1, 3):
        for half in range(2):
            push(line(half), 1 + half, 1 + half, to_first[half](d))
    for half in range(2):
        settle(three_lines, recv.at[1 + half])
        for d in (2, 1, 3):
            push(unit(half, second[half](0)), 3 + half, 4 + 3 * half + d, to_second[half](d))
    for half in range(2):
        push(unit(half, second[half](0)), 5 + half, 3 + half * 8, me.device(core=1 - c))
    for d in (1, 3, 2):
        for half in range(2):
            spot = unit(half, second[half](4 - d))
            settle(out.at[spot], recv.at[4 + 3 * half + d])
            push(spot, 5 + half, 3 + half * 8, me.device(core=1 - c))
    for half in range(2):
        settle(out.at[half, :, :, 1 - c], recv.at[3 + half * 8])

    def drain():
        settle(seven, send.at[0])
        for half in range(2):
            settle(three_lines, send.at[1 + half])
            settle(three_units, send.at[3 + half])
            settle(out.at[half, :, :, c], send.at[5 + half])

    return drain


def split(value):
    high = value.astype(BF16)
    return high, (value - high.astype(F32)).astype(BF16)


def dot(left, right):
    return jnp.dot(left, right, preferred_element_type=F32)


def times(a, b):
    return (a[0] * b[0] - a[1] * b[1], a[0] * b[1] + a[1] * b[0])


def conj_times(a, b):
    return (a[0] * b[0] + a[1] * b[1], a[0] * b[1] - a[1] * b[0])


def kernel(factor, offsets_ref, order_ref, block_ref, probe_hbm, phase_hbm, measured_hbm, table_hbm, out_ref,
           whole, probe_ref, phase_ref, measured_ref, table_ref, medium, slab, windows, waves, pend, place_ref,
           grads, inbox, acc, hop, ring, line, piece, stage, box, final,
           load_sem, send, recv, s1_send, s1_recv, hop_send, hop_recv, ring_send, ring_recv, line_send, line_recv,
           end_send, end_recv):
    layers = order_ref.shape[0]
    count, length = measured_ref.shape[:2]
    lanes = whole.shape[-1]
    field = 2 * lanes
    me = Place()
    x, y, c = me.x, me.y, me.core
    other = 1 - c
    loads = [
        pltpu.make_async_copy(src, dst, load_sem.at[i])
        for i, (src, dst) in enumerate((
            (phase_hbm, phase_ref), (probe_hbm, probe_ref), (table_hbm, table_ref), (measured_hbm, measured_ref)))
    ]
    for load in loads:
        load.start()
    for row in range(block_ref.shape[1]):
        for half in range(2):
            whole[half, me.depth, me.yz, c, 2 * row:2 * row + 2] = block_ref[0, row, :, half * lanes:(half + 1) * lanes]
    greet(me)
    lane = lax.broadcasted_iota(jnp.int32, (length, lanes), 1)

    def prepare():
        for load in loads:
            load.wait()
        medium[0] = jnp.cos(phase_ref[...])
        medium[1] = jnp.sin(phase_ref[...])
        rows = lax.broadcasted_iota(jnp.int32, (field, length), 0)
        inner = lax.broadcasted_iota(jnp.int32, (field, length), 1)
        for p in range(count):
            hit = rows - inner == offsets_ref[0, p]
            place_ref[:, p * length:(p + 1) * length] = jnp.where(hit, 1.0, 0.0).astype(BF16)
            waves[0, p] = probe_ref[...]

    drain_gather = gather_whole(me, whole, send, recv, prepare)

    def right_map(blocks, which):
        high_table, low_table = table_ref[which, 0], table_ref[which, 1]
        results = []
        for block in blocks:
            high, low = split(jnp.concatenate(block, axis=1))
            out = dot(high, high_table) + (dot(low, high_table) + dot(high, low_table))
            results.append((out[:, :length], out[:, length:]))
        return results

    def left_map(blocks, which):
        high_table, low_table = table_ref[which, 0], table_ref[which, 1]
        stacked = jnp.concatenate([jnp.concatenate(block, axis=0) for block in blocks], axis=1)
        high, low = split(stacked)
        out = dot(high_table, high) + (dot(high_table, low) + dot(low_table, high))
        return [
            (out[:length, i * length:(i + 1) * length], out[length:, i * length:(i + 1) * length])
            for i in range(len(blocks))
        ]

    def forward(blocks):
        return left_map(right_map(blocks, 0), 1)

    def inverse(blocks):
        return left_map(right_map(blocks, 1), 0)

    def load_windows(layer):
        index = order_ref[layer]
        for half in range(2):
            slab[half] = whole[half, index].reshape(2 * field, lanes).astype(F32)
        for p in range(count):
            row, column = offsets_ref[0, p], offsets_ref[1, p]
            shift = lax.rem(lanes - column, lanes)
            keep = lane < lanes - column
            for part in range(2):
                left = slab[0, pl.ds(2 * row + part, length, stride=2), :]
                right = slab[1, pl.ds(2 * row + part, length, stride=2), :]
                windows[layer, p, part] = jnp.where(keep, pltpu.roll(left, shift, 1), pltpu.roll(right, shift, 1))

    def window_of(layer, p):
        return windows[layer, p, 0], windows[layer, p, 1]

    def wave_of(layer, p):
        return waves[layer, p, 0], waves[layer, p, 1]

    def add_grads(j, slot):
        layer = layers - 1 - j
        terms = [conj_times(wave_of(layer, p), (pend[slot, p, 0], pend[slot, p, 1])) for p in range(count)]
        for part in range(2):
            moved = []
            for p in range(count):
                column = offsets_ref[1, p]
                turned = pltpu.roll(terms[p][part], lax.rem(column, lanes), 1)
                moved.append(jnp.concatenate(
                    [jnp.where(lane >= column, turned, 0.0), jnp.where(lane >= column, 0.0, turned)], axis=1))
            high, low = split(jnp.concatenate(moved, axis=0))
            total = dot(place_ref[...], high) + dot(place_ref[...], low)
            for half in range(2):
                grads[j, half, part] = total[:, half * lanes:(half + 1) * lanes].reshape(Y * ZL, 2, 8, lanes)

    def y_unit(d):
        return pl.ds(ZL * me.ys(d), ZL)

    def do_share(j):
        remote(grads.at[j, :, :, :, other], inbox.at[j], s1_send.at[0], s1_recv.at[j], me.device(core=other)).start()

    def do_fold(j):
        settle(inbox.at[j], s1_recv.at[j])
        acc[j] = grads[j, :, :, :, c] + inbox[j]
        for side in range(2):
            remote(acc.at[j, side, :, y_unit(2)], hop.at[j, side], hop_send.at[0], hop_recv.at[j, side],
                   me.device(y=me.ys(1 + 2 * side))).start()

    def do_ring(j):
        for side in range(2):
            unit = y_unit(1 + 2 * side)
            settle(hop.at[j, side], hop_recv.at[j, side])
            acc[j, side, :, unit] = acc[j, side, :, unit] + hop[j, side]
            remote(acc.at[j, :, :, unit], ring.at[j, side], ring_send.at[0], ring_recv.at[j, side],
                   me.device(y=me.ys(1 + 2 * side))).start()

    def do_line(j):
        for side in range(2):
            settle(ring.at[j, side], ring_recv.at[j, side])
        acc[j, :, :, y_unit(0)] = acc[j, :, :, y_unit(0)] + ring[j, 0] + ring[j, 1]
        for d in (2, 3, 1):
            zl = (me.zl + d) % ZL
            remote(acc.at[j, :, :, ZL * y + zl], line.at[j, d - 1], line_send.at[0], line_recv.at[j],
                   me.device(z=me.zh * ZL + zl)).start()

    def do_piece(j):
        settle(line.at[j], line_recv.at[j])
        piece[j] = acc[j, :, :, me.yz] + line[j, 0] + line[j, 1] + line[j, 2]

    load_windows(0)

    @pl.loop(0, layers - 1, unroll=7)
    def _(layer):
        load_windows(layer + 1)
        field_factor = (medium[0], medium[1])
        blocks = [times(window_of(layer, p), wave_of(layer, p)) for p in range(count)]
        blocks = [times(b, field_factor) for b in forward(blocks)]
        for p, block in enumerate(inverse(blocks)):
            waves[layer + 1, p, 0] = block[0]
            waves[layer + 1, p, 1] = block[1]

    last = layers - 1
    blocks = [times(window_of(last, p), wave_of(last, p)) for p in range(count)]
    scaled = []
    for p, block in enumerate(forward(blocks)):
        miss = (2.0 * factor) * (block[0] * block[0] + block[1] * block[1] - measured_ref[p])
        scaled.append((miss * block[0], miss * block[1]))
    for p, block in enumerate(inverse(scaled)):
        pend[0, p, 0] = block[0]
        pend[0, p, 1] = block[1]

    @pl.loop(0, layers - 1)
    def _(i):
        @pl.when(i >= LINE)
        def _():
            do_line(i - LINE)

        @pl.when(i >= RING)
        def _():
            do_ring(i - RING)

        @pl.when(i >= 3)
        def _():
            do_fold(i - 3)

        @pl.when(i >= 1)
        def _():
            do_share(i - 1)

        slot = lax.rem(i, 2)
        layer = layers - 2 - i
        field_factor = (medium[0], medium[1])
        blocks = [conj_times(window_of(layer + 1, p), (pend[slot, p, 0], pend[slot, p, 1])) for p in range(count)]
        blocks = [conj_times(field_factor, b) for b in forward(blocks)]
        blocks = inverse(blocks)
        add_grads(i, slot)
        for p, block in enumerate(blocks):
            pend[1 - slot, p, 0] = block[0]
            pend[1 - slot, p, 1] = block[1]

    do_share(6)
    add_grads(7, 1)
    do_share(7)
    do_fold(4)
    do_fold(5)
    for j in range(7 - RING, 4):
        do_ring(j)
    do_fold(6)
    drain_gather()
    do_fold(7)
    do_ring(4)
    do_ring(5)
    for j in range(7 - LINE, 3):
        do_line(j)
    do_ring(6)
    do_line(3)
    do_line(4)
    do_ring(7)
    do_line(5)
    do_line(6)
    for j in range(5):
        do_piece(j)
    do_line(7)
    for j in range(5, 8):
        do_piece(j)

    for s in range(layers):
        inverse_index = jnp.zeros((), jnp.int32)
        for k in range(layers):
            inverse_index = jnp.where(order_ref[k] == s, layers - 1 - k, inverse_index)
        stage[s] = piece[inverse_index]
    for i, (dx, dz) in enumerate(DEPTH_STEPS):
        target = me.xs(dx) * ZH + me.zs(dz) // ZL
        remote(stage.at[target], box.at[i], end_send.at[0], end_recv.at[0],
               me.device(x=me.xs(dx), z=me.zs(dz))).start()
    settle(inbox, s1_send.at[0])
    settle(hop, hop_send.at[0])
    settle(ring, ring_send.at[0])
    settle(line, line_send.at[0])
    settle(box, end_recv.at[0])
    total = stage[me.depth]
    for i in range(len(DEPTH_STEPS)):
        total = total + box[i]
    for half in range(2):
        for part in range(2):
            final[half, pl.ds(part, 8, stride=2), :] = total[half, part]
        out_ref[:, half * lanes:(half + 1) * lanes] = final[half]
    settle(box, end_send.at[0])


def per_device(object_slices, probe_wave, propagator_phase, measured, offsets, slice_order):
    layers = slice_order.shape[0]
    width = object_slices.shape[3]
    length = probe_wave.shape[1]
    count = offsets.shape[0]
    positions_total = count * lax.axis_size("depth") * lax.axis_size("pos")
    factor = 0.25 * width / (length * math.sqrt(positions_total))
    table = jnp.asarray(dft_tables(length))
    vmem = pl.BlockSpec(memory_space=pltpu.VMEM)
    smem = pl.BlockSpec(memory_space=pltpu.SMEM)
    anywhere = pl.BlockSpec(memory_space=pl.ANY)
    dma = pltpu.SemaphoreType.DMA
    block = (2, 2, 8, 128)
    total = pl.pallas_call(
        functools.partial(kernel, factor),
        out_shape=jax.ShapeDtypeStruct((16, width), F32),
        in_specs=[smem, smem, vmem] + [anywhere] * 4,
        out_specs=vmem,
        scratch_shapes=[
            pltpu.VMEM((2, layers, Y * ZL, 2, 16, 128), BF16),
            pltpu.VMEM((2, length, length), F32),
            pltpu.VMEM((length, length), F32),
            pltpu.VMEM((count, length, length), F32),
            pltpu.VMEM((2, 2, 2 * length, 2 * length), BF16),
            pltpu.VMEM((2, length, length), F32),
            pltpu.VMEM((2, 2 * width, 128), F32),
            pltpu.VMEM((layers, count, 2, length, length), F32),
            pltpu.VMEM((layers, count, 2, length, length), F32),
            pltpu.VMEM((2, count, 2, length, length), F32),
            pltpu.VMEM((width, count * length), BF16),
            pltpu.VMEM((layers, 2, 2, Y * ZL, 2, 8, 128), F32),
            pltpu.VMEM((layers, 2, 2, Y * ZL, 8, 128), F32),
            pltpu.VMEM((layers, 2, 2, Y * ZL, 8, 128), F32),
            pltpu.VMEM((layers, 2, 2, ZL, 8, 128), F32),
            pltpu.VMEM((layers, 2, 2, 2, ZL, 8, 128), F32),
            pltpu.VMEM((layers, 3) + block, F32),
            pltpu.VMEM((layers,) + block, F32),
            pltpu.VMEM((layers,) + block, F32),
            pltpu.VMEM((7,) + block, F32),
            pltpu.VMEM((2, 16, 128), F32),
            dma((4,)), dma((7,)), dma((12,)),
            dma((1,)), dma((layers,)), dma((1,)), dma((layers, 2)), dma((1,)), dma((layers, 2)),
            dma((1,)), dma((layers,)), dma((2,)), dma((2,)),
        ],
        compiler_params=pltpu.CompilerParams(collective_id=0, has_side_effects=True, vmem_limit_bytes=56 * 2**20),
    )(offsets.T, slice_order, object_slices, probe_wave, propagator_phase, measured, table)
    return total.reshape(object_slices.shape)


def solution(mesh):
    in_specs = (
        P("depth", "pos", None, None),
        P(),
        P(),
        P(("depth", "pos"), None, None),
        P(("depth", "pos"), None),
        P(),
    )
    out_specs = P("depth", "pos", None, None)
    return jax.shard_map(
        per_device, mesh=mesh, in_specs=in_specs, out_specs=out_specs, check_vma=False
    )
```
